256 devices in a mesh: seq: 64 (over z, y, core), head: 4 (over x).
Axes of the slice: x: 4, y: 4, z: 8, core: 2. Of those that a mesh axis runs over, the one named last changes fastest.
Arguments:
- inputs: bfloat16 [131072, 4096], P('seq', 'head'), may hold values from -6 to 6
- state_in: bfloat16 [131072, 128], P('seq'), may hold values from -6 to 6
- state_out: bfloat16 [131072, 128], P('seq'), may hold values from -0.046875 to 0.046875
- log_decay: float32 [64, 131072], P('head', 'seq'), may hold values from -0.6 to 0, as said below
- level_weight: float32 [7, 64, 131072], P(None, 'head', 'seq'), may hold values from 0.25 to 2
- skip: float32 [64], P('head'), may hold values from 0.5 to 1.5
- norm_gain: float32 [4096], P('head'), may hold values from 0.25 to 1.75
- resets: int32 [4], replicated, may hold values from 1 to 131071
Outputs:
- mixed: bfloat16 [131072, 4096], P('seq', 'head')
The draws below stay inside these ranges and needn't reach their ends.
Inputs may be any that keep to these rules, and one draw needn't show every extreme that they name: `log_decay`: natural logarithm of a decay factor; every value is below zero. `resets`: positions may repeat.
All inputs are finite; a program needn't handle non-finite values.
Results may differ from the reference program's by a relative error of at most 0.005.
Values may be sent and summed in bfloat16 or wider, within the bound.
No kernel may reach another device: no remote copies, remote signals or barrier semaphores. Data moves between devices by JAX's collectives and lax.ppermute only.
A program may use at most 128 MiB of HBM per device.

```python
import math
import jax
import jax.numpy as jnp
from jax import lax

HEAD_TOTAL = 64
HEAD_DIM = 64
STATE = 128
BLOCK = 256
LEVELS = 7
RESETS = 4
TOK_DEV = 2048
TOKEN_TOTAL = 131072


def draw_log_decay(key, part):
    key = jax.random.fold_in(key, 17)
    key_rows = jax.random.split(key, 7)
    fast_share = 0.5
    coarse_estimate = jnp.exp(jax.random.uniform(key_rows[0], (HEAD_TOTAL, TOKEN_TOTAL), minval=-0.55, maxval=0.4))
    fast = jax.random.uniform(key_rows[1], (HEAD_TOTAL, 1)) < fast_share
    fast_rate = jnp.exp(-jax.random.uniform(key_rows[2], (HEAD_TOTAL, 1), minval=math.log(30.0), maxval=math.log(50.0)))
    slow_rate = jnp.exp(jax.random.uniform(key_rows[3], (HEAD_TOTAL, 1), minval=math.log(0.1), maxval=math.log(0.4))) / TOKEN_TOTAL
    baseline_decay_rate = jnp.where(fast, fast_rate, slow_rate)
    device_factor = jnp.exp(jax.random.uniform(key_rows[4], (HEAD_TOTAL, TOKEN_TOTAL // TOK_DEV, 1), minval=-0.45, maxval=0.45))
    multiplier_term = jnp.broadcast_to(device_factor, (HEAD_TOTAL, TOKEN_TOTAL // TOK_DEV, TOK_DEV)).reshape(HEAD_TOTAL, TOKEN_TOTAL)
    spots = jax.random.randint(key_rows[5], (HEAD_TOTAL, 3), 0, TOKEN_TOTAL)
    reset_hit_flags = jnp.any(jnp.arange(TOKEN_TOTAL, dtype=jnp.int32)[None, :, None] == spots[:, None, :], axis=2)
    sudden_spike = jax.random.uniform(key_rows[6], (HEAD_TOTAL, TOKEN_TOTAL), minval=-0.45, maxval=-0.22)
    value_rows = -baseline_decay_rate * multiplier_term * coarse_estimate + jnp.where(reset_hit_flags, sudden_spike, 0.0)
    return value_rows.astype(jnp.float32)


def set_ends(array, key, low, top_value):
    spot = [jax.random.randint(jax.random.fold_in(key, axis), (), 0, length) for axis, length in enumerate(array.shape)]
    main_axis = array.shape.index(max(array.shape))
    beside = spot[:main_axis] + [(spot[main_axis] + 1) % array.shape[main_axis]] + spot[main_axis + 1:]
    return array.at[tuple(spot)].set(low).at[tuple(beside)].set(top_value)


def level_of(own_key, extent, shards, smallest, high):
    loudness = 1.0
    for position, shards_of in shards:
        steps = jax.random.uniform(jax.random.fold_in(jax.random.fold_in(own_key, 6), position), (shards_of,), jnp.float32, smallest / len(shards), high / len(shards))
        loudness = loudness * jnp.repeat(jnp.exp(steps), extent[position] // shards_of).reshape((-1,) + (1,) * (len(extent) - 1 - position))
    return loudness


def normal_values(key, extent, width, most, cuts=(), kind=jnp.bfloat16):
    values = jax.random.normal(key, extent, jnp.float32) * width
    if len(cuts) > 0:
        values = level_of(key, extent, cuts, -0.22, 0.18) * values
    return jnp.clip(values, min=-most, max=most).astype(kind)


def setup_inputs(seed: int = 0) -> dict:
    keys = jax.random.split(jax.random.key(seed), 9)
    return {
        "inputs": normal_values(keys[0], (TOKEN_TOTAL, HEAD_TOTAL * HEAD_DIM), 1.0, 6.0, ((0, 64), (1, 4))),
        "state_in": normal_values(keys[1], (TOKEN_TOTAL, STATE), 1.0, 6.0, ((0, 64),)),
        "state_out": normal_values(keys[2], (TOKEN_TOTAL, STATE), (STATE * STATE) ** -0.5, 0.046875, ((0, 64),)),
        "log_decay": draw_log_decay(jax.random.fold_in(keys[8], 71), 0),
        "level_weight": jnp.clip(jnp.exp(math.log(2.0) - 2.0794415 * jax.random.uniform(keys[4], (LEVELS, HEAD_TOTAL, TOKEN_TOTAL), jnp.float32) ** level_of(keys[4], (LEVELS, HEAD_TOTAL, TOKEN_TOTAL), ((1, 4), (2, 64)), -0.2, 0.2)), 0.25, 2.0),
        "skip": jnp.clip(0.5 + 1.0 * jax.random.uniform(keys[5], (HEAD_TOTAL,), jnp.float32) ** level_of(keys[5], (HEAD_TOTAL,), ((0, 4),), -0.2, 0.2), 0.5, 1.5),
        "norm_gain": jnp.clip(1.0 + 0.15 * jax.random.normal(keys[6], (HEAD_TOTAL * HEAD_DIM,), jnp.float32), 0.25, 1.75),
        "resets": set_ends(jax.random.randint(keys[7], (RESETS,), 1, TOKEN_TOTAL), jax.random.fold_in(keys[7], 1), 1, TOKEN_TOTAL - 1).astype(jnp.int32),
    }


EPSILON = 1e-05

def running_sums(log_rate, flags):
    return (jnp.cumsum(log_rate, axis=1), jnp.cumsum(flags, dtype=jnp.int32))

def level_rank(distance):
    rank = jnp.zeros_like(distance)
    for bit_number in range(LEVELS - 1):
        rank = rank + (jnp.right_shift(distance, bit_number) > 0).astype(jnp.int32)
    return rank

def stretch_state(running_log, reset_count, state_part, inputs_part):
    weight = jnp.where((reset_count == reset_count[-1])[None, :], jnp.exp(running_log[:, -1:] - running_log), 0.0)
    scaled = (weight[:, :, None] * state_part.astype(jnp.float32)[None]).astype(jnp.bfloat16)
    return jnp.einsum('hsn,shp->hnp', scaled.astype(jnp.float32), inputs_part.astype(jnp.float32), precision=lax.Precision.HIGHEST)

def block_states(running_log, reset_count, state_blocks, input_blocks, stretch_count):
    heads_here = running_log.shape[0]
    log_stretches = running_log.reshape(heads_here, stretch_count, BLOCK).transpose(1, 0, 2)
    count_stretches = reset_count.reshape(stretch_count, BLOCK)

    def one_state(packed):
        return stretch_state(packed[0], packed[1], packed[2], packed[3])
    states = lax.map(one_state, (log_stretches, count_stretches, state_blocks, input_blocks))
    end_logs = log_stretches[:, :, -1]
    end_counts = count_stretches[:, -1]
    prev_ends = jnp.concatenate([jnp.zeros_like(end_logs[:1]), end_logs[:-1]], 0)
    prev_counts = jnp.concatenate([jnp.zeros_like(end_counts[:1]), end_counts[:-1]], 0)
    order = jnp.arange(stretch_count, dtype=jnp.int32)
    valid = (order[None, :] < order[:, None]) & (prev_counts[:, None] == end_counts[None, :])
    exponent = jnp.where(valid[:, :, None], prev_ends[:, None, :] - end_logs[None, :, :], -jnp.inf)
    starts = jnp.einsum('ckh,khnp->chnp', jnp.exp(exponent), states, precision=lax.Precision.HIGHEST)
    final = jnp.where((end_counts == end_counts[-1])[:, None], jnp.exp(end_logs[-1][None, :] - end_logs), 0.0)
    block_total = jnp.einsum('kh,khnp->hnp', final, states, precision=lax.Precision.HIGHEST)
    return (starts, block_total, prev_ends, prev_counts)

def stretch_output(running_log, reset_count, level_coef, prev_end, prev_count, stretch_start, state_part, out_part, inputs_part, level_low, skip):
    offsets = jnp.arange(BLOCK, dtype=jnp.int32)
    causal = (offsets[None, :] <= offsets[:, None]) & (reset_count[None, :] == reset_count[:, None])
    exponent = jnp.where(causal[None], running_log[:, :, None] - running_log[:, None, :], -jnp.inf)
    decay = jnp.exp(exponent) * level_coef[0][:, :, None]
    scores = jnp.dot(out_part.astype(jnp.float32), state_part.astype(jnp.float32).T, precision=lax.Precision.HIGHEST)
    mask_weight = (decay * scores[None]).astype(jnp.bfloat16)
    inner = jnp.einsum('hts,shp->thp', mask_weight.astype(jnp.float32), inputs_part.astype(jnp.float32), precision=lax.Precision.HIGHEST)
    stacked = jnp.concatenate([stretch_start.astype(jnp.bfloat16)[None], level_low], 0)
    reads = jnp.einsum('tn,lhnp->tlhp', out_part.astype(jnp.float32), stacked.astype(jnp.float32), precision=lax.Precision.HIGHEST)
    near = jnp.where((reset_count == prev_count)[None, :], jnp.exp(running_log - prev_end[:, None]), 0.0)
    far_side = jnp.where((reset_count == 0)[None, :], jnp.exp(running_log), 0.0)
    multiplier_term = level_coef * jnp.concatenate([near[None], jnp.broadcast_to(far_side[None], (LEVELS - 1,) + far_side.shape)], 0)
    carried = jnp.einsum('lht,tlhp->thp', multiplier_term, reads, precision=lax.Precision.HIGHEST)
    return inner + carried + skip[None, :, None] * inputs_part.astype(jnp.float32)

def level_states(block_index, totals, log_totals, clears):
    block_count = totals.shape[0]
    cum_log = jnp.cumsum(log_totals, axis=0)
    cum_clear = jnp.cumsum(clears, dtype=jnp.int32)
    source = jnp.arange(block_count, dtype=jnp.int32)
    before = jnp.maximum(block_index - 1, 0)
    valid = (source < block_index) & (cum_clear[before] == cum_clear)
    exponent = jnp.where(valid[:, None], cum_log[before][None, :] - cum_log, -jnp.inf)
    weight = jnp.exp(exponent)
    rank = level_rank(jnp.bitwise_xor(block_index, source))
    select = (rank[None, :] == jnp.arange(1, LEVELS, dtype=jnp.int32)[:, None]).astype(jnp.float32)
    mixing = select[:, :, None] * weight[None]
    return jnp.einsum('ljh,jhnp->lhnp', mixing, totals, precision=lax.Precision.HIGHEST)

def reference(inputs, state_in, state_out, log_decay, level_weight, skip, norm_gain, resets):
    stretch_count = TOK_DEV // BLOCK
    block_count = TOKEN_TOTAL // TOK_DEV
    input_all = inputs.reshape(block_count, stretch_count, BLOCK, HEAD_TOTAL, HEAD_DIM)
    in_all = state_in.reshape(block_count, stretch_count, BLOCK, STATE)
    out_all = state_out.reshape(block_count, stretch_count, BLOCK, STATE)
    rates = log_decay.reshape(HEAD_TOTAL, block_count, TOK_DEV).transpose(1, 0, 2)
    coefs = level_weight.reshape(LEVELS, HEAD_TOTAL, block_count, TOK_DEV).transpose(2, 0, 1, 3)
    flags = jnp.zeros((TOKEN_TOTAL,), jnp.int32).at[resets].set(1).reshape(block_count, TOK_DEV)

    def first_pass(packed):
        rate_block, flag_block, in_block, input_block = packed
        running_log, reset_count = running_sums(rate_block, flag_block)
        starts, block_total, prev_ends, prev_counts = block_states(running_log, reset_count, in_block, input_block, stretch_count)
        return (block_total, running_log[:, -1], reset_count[-1])
    totals, log_totals, clears = lax.map(first_pass, (rates, flags, in_all, input_all))

    def second_pass(packed):
        block_index, rate_block, flag_block, coef_block, in_block, out_block, input_block = packed
        running_log, reset_count = running_sums(rate_block, flag_block)
        starts, block_total, prev_ends, prev_counts = block_states(running_log, reset_count, in_block, input_block, stretch_count)
        level_low = level_states(block_index, totals, log_totals, clears).astype(jnp.bfloat16)
        log_stretches = running_log.reshape(HEAD_TOTAL, stretch_count, BLOCK).transpose(1, 0, 2)
        count_stretches = reset_count.reshape(stretch_count, BLOCK)
        coef_stretches = coef_block.reshape(LEVELS, HEAD_TOTAL, stretch_count, BLOCK).transpose(2, 0, 1, 3)

        def one_stretch(parts):
            return stretch_output(parts[0], parts[1], parts[2], parts[3], parts[4], parts[5], parts[6], parts[7], parts[8], level_low, skip)
        value_rows = lax.map(one_stretch, (log_stretches, count_stretches, coef_stretches, prev_ends, prev_counts, starts, in_block, out_block, input_block))
        mean_square = lax.optimization_barrier(jnp.mean(value_rows * value_rows, axis=(2, 3), keepdims=True))
        scaled = value_rows * lax.rsqrt(mean_square + EPSILON) * norm_gain.reshape(HEAD_TOTAL, HEAD_DIM)
        return scaled.astype(jnp.bfloat16).reshape(TOK_DEV, HEAD_TOTAL * HEAD_DIM)
    result = lax.map(second_pass, (jnp.arange(block_count, dtype=jnp.int32), rates, flags, coefs, in_all, out_all, input_all))
    return result.reshape(TOKEN_TOTAL, HEAD_TOTAL * HEAD_DIM)
```

```python
import functools

import jax
import jax.numpy as jnp
from jax import lax
from jax.experimental import pallas as pl
from jax.experimental.pallas import tpu as pltpu
from jax.sharding import PartitionSpec as P

HEAD_TOTAL = 64
HEAD_DIM = 64
STATE = 128
LEVELS = 7
TOK_DEV = 2048
EPSILON = 1e-05

CHUNK = 256
CHUNKS = TOK_DEV // CHUNK
HEADS = 16
FEATURES = HEADS * HEAD_DIM
HALF = FEATURES // 2
PAIRS = HEADS // 2
WIDE = 2 * HEAD_DIM
SPAN_ROWS = 3 * HEADS
RESETS = 4
STEPS = ((2, 1), (6, 2), (8, 3), (16, 4), (48, 5))
PIECE = 2

F32 = jnp.float32
BF16 = jnp.bfloat16
PARAMS = dict(vmem_limit_bytes=32 * 1024 * 1024)


def dot(a, b):
    return lax.dot_general(a, b, (((1,), (0,)), ((), ())), preferred_element_type=F32)


def dot_nt(a, b):
    return lax.dot_general(a, b, (((1,), (1,)), ((), ())), preferred_element_type=F32)


def pair_rows(values, pair):
    width = values.shape[1]
    return jnp.concatenate(
        [
            jnp.broadcast_to(values[h : h + 1, :], (HEAD_DIM, width))
            for h in (2 * pair, 2 * pair + 1)
        ],
        axis=0,
    )


def pair_column(values, pair, width):
    return jnp.concatenate(
        [
            jnp.broadcast_to(values[h : h + 1, 0:1], (HEAD_DIM, width))
            for h in (2 * pair, 2 * pair + 1)
        ],
        axis=0,
    )


def write_spans(ref, first, span):
    high = span.astype(BF16)
    rest = span - high.astype(F32)
    middle = rest.astype(BF16)
    low = (rest - middle.astype(F32)).astype(BF16)
    ref[first : first + SPAN_ROWS, :] = jnp.concatenate([high, middle, low], axis=0)


def read_spans(ref, first):
    parts = ref[first : first + SPAN_ROWS, :].astype(F32)
    return parts[:HEADS] + parts[HEADS : 2 * HEADS] + parts[2 * HEADS :]


def state_kernel(
    place, resets, x_ref, b_ref, decay_ref, total_ref, pay_ref, start_ref, log_ref, far_ref, span_ref, state, logs
):
    c = pl.program_id(0)
    base = place[0] * TOK_DEV

    @pl.when(c == 0)
    def _():
        state[...] = jnp.zeros_like(state)
        rows = jnp.concatenate(
            [decay_ref[:, k * CHUNK : (k + 1) * CHUNK] for k in range(CHUNKS)], axis=0
        )
        square = (CHUNK, CHUNK)
        upto = lax.broadcasted_iota(jnp.int32, square, 0) <= lax.broadcasted_iota(
            jnp.int32, square, 1
        )
        ones = upto.astype(F32).astype(BF16)
        high = rows.astype(BF16)
        rest = rows - high.astype(F32)
        middle = rest.astype(BF16)
        low = (rest - middle.astype(F32)).astype(BF16)
        sums = dot(high, ones) + dot(middle, ones) + dot(low, ones)
        before = jnp.zeros((HEADS, 1), F32)
        for k in range(CHUNKS):
            part = sums[k * HEADS : (k + 1) * HEADS]
            logs[k] = part
            log_ref[:, k * CHUNK : (k + 1) * CHUNK] = part
            position = base + k * CHUNK + lax.broadcasted_iota(jnp.int32, (HEADS, CHUNK), 1)
            far = jnp.exp(before + part)
            for r in range(RESETS):
                cut = (resets[r] >= base) & (position >= resets[r])
                far = jnp.where(cut, 0.0, far)
            far_ref[:, k * CHUNK : (k + 1) * CHUNK] = far
            before = before + part[:, CHUNK - 1 : CHUNK]
            if k == CHUNKS - 1:
                span_ref[...] = jnp.broadcast_to(far[:, CHUNK - 1 : CHUNK], (HEADS, STATE))

    log = logs[c]
    end = log[:, CHUNK - 1 : CHUNK]
    first = base + c * CHUNK
    last = first + CHUNK - 1
    position = first + lax.broadcasted_iota(jnp.int32, (HEADS, CHUNK), 1)
    weight = jnp.exp(end - log)
    kept = jnp.exp(end)
    for r in range(RESETS):
        weight = jnp.where((position < resets[r]) & (resets[r] <= last), 0.0, weight)
        kept = jnp.where((resets[r] >= first) & (resets[r] <= last), 0.0, kept)
    middle = jnp.exp(0.5 * end)
    b = b_ref[...]
    for pair in range(PAIRS):
        rows = slice(pair * WIDE, (pair + 1) * WIDE)
        held = state[rows, :]
        start_ref[0, rows, :] = (held * pair_column(middle, pair, STATE)).astype(BF16)
        flipped = x_ref[:, rows].T
        scaled = (flipped.astype(F32) * pair_rows(weight, pair)).astype(BF16)
        state[rows, :] = held * pair_column(kept, pair, STATE) + dot(scaled, b)

    @pl.when(c == CHUNKS - 1)
    def _():
        total = state[...]
        total_ref[...] = total
        pay_ref[:FEATURES, :] = total.astype(BF16)
        write_spans(pay_ref, FEATURES, span_ref[...])


def whole(shape):
    return pl.BlockSpec(shape, lambda *_: (0,) * len(shape))


SMEM = pl.BlockSpec(memory_space=pltpu.SMEM)


def block_states(place, resets, inputs, state_in, log_decay):
    return pl.pallas_call(
        state_kernel,
        grid=(CHUNKS,),
        in_specs=[
            SMEM,
            SMEM,
            pl.BlockSpec((CHUNK, FEATURES), lambda c: (c, 0)),
            pl.BlockSpec((CHUNK, STATE), lambda c: (c, 0)),
            whole((HEADS, TOK_DEV)),
        ],
        out_specs=[
            whole((FEATURES, STATE)),
            whole((FEATURES + SPAN_ROWS, STATE)),
            pl.BlockSpec((1, FEATURES, STATE), lambda c: (c, 0, 0)),
            whole((HEADS, TOK_DEV)),
            whole((HEADS, TOK_DEV)),
            whole((HEADS, STATE)),
        ],
        out_shape=[
            jax.ShapeDtypeStruct((FEATURES, STATE), F32),
            jax.ShapeDtypeStruct((FEATURES + SPAN_ROWS, STATE), BF16),
            jax.ShapeDtypeStruct((CHUNKS, FEATURES, STATE), BF16),
            jax.ShapeDtypeStruct((HEADS, TOK_DEV), F32),
            jax.ShapeDtypeStruct((HEADS, TOK_DEV), F32),
            jax.ShapeDtypeStruct((HEADS, STATE), F32),
        ],
        scratch_shapes=[
            pltpu.VMEM((FEATURES, STATE), F32),
            pltpu.VMEM((CHUNKS, HEADS, CHUNK), F32),
        ],
        compiler_params=pltpu.CompilerParams(**PARAMS),
        name="block_states",
    )(place, resets, inputs, state_in, log_decay)


def join_kernel(shift, first, place, own_ref, span_ref, lead_ref, got_ref, *outs):
    sum_ref, new_span_ref, new_lead_ref, factor_ref, pay_ref = outs
    core = place[1]
    upper = place[2 + shift] == 1
    top = FEATURES if first else HALF
    span = span_ref[...]
    got_span = read_spans(got_ref, top)
    lead = lead_ref[...]
    factor_ref[...] = jnp.where(upper, lead, 0.0)
    new_lead_ref[...] = jnp.where(upper, lead * got_span, lead)
    both = span * got_span
    new_span_ref[...] = both
    span_here = jnp.where(core == 0, span[: HEADS // 2], span[HEADS // 2 :])
    got_here = jnp.where(core == 0, got_span[: HEADS // 2], got_span[HEADS // 2 :])
    own_factor = jnp.where(upper, 1.0, got_here)
    got_factor = jnp.where(upper, span_here, 1.0)
    offset = core * HALF if first else 0
    for h in range(HEADS // 2):
        rows = pl.ds(pl.multiple_of(offset + h * HEAD_DIM, HEAD_DIM), HEAD_DIM)
        new = own_ref[rows, :] * own_factor[h : h + 1] + got_ref[rows, :].astype(F32) * got_factor[
            h : h + 1
        ]
        here = slice(h * HEAD_DIM, (h + 1) * HEAD_DIM)
        sum_ref[here, :] = new
        pay_ref[here, :] = new.astype(BF16)
    write_spans(pay_ref, HALF, both)


def join(shift, first, place, own, span, lead, got):
    small = jax.ShapeDtypeStruct((HEADS, STATE), F32)
    vmem = pl.BlockSpec(memory_space=pltpu.VMEM)
    return pl.pallas_call(
        functools.partial(join_kernel, shift, first),
        in_specs=[SMEM] + [vmem] * 4,
        out_specs=[vmem] * 5,
        out_shape=[
            jax.ShapeDtypeStruct((HALF, STATE), F32),
            small,
            small,
            small,
            jax.ShapeDtypeStruct((HALF + SPAN_ROWS, STATE), BF16),
        ],
        compiler_params=pltpu.CompilerParams(**PARAMS),
        name="join" + str(shift),
    )(place, own, span, lead, got)


def inner_kernel(
    chunk0, place, resets, skip, x_ref, b_ref, c_ref, log_ref, weight_ref, far_ref, start_ref, got_ref, factor_ref, *rest
):
    y_ref = rest[-1]
    first = place[0] * TOK_DEV + (pl.program_id(0) + chunk0) * CHUNK
    log = log_ref[...]
    middle = 0.5 * log[:, CHUNK - 1 : CHUNK]
    after = weight_ref[0] * jnp.exp(log - middle)
    before = jnp.exp(middle - log)
    level = weight_ref[1] * far_ref[...] * factor_ref[:, 0:1]
    square = (CHUNK, CHUNK)
    source = first + lax.broadcasted_iota(jnp.int32, square, 0)
    target = first + lax.broadcasted_iota(jnp.int32, square, 1)
    scores = dot_nt(b_ref[...], c_ref[...])
    scores = jnp.where(source <= target, scores, 0.0)
    row = first + lax.broadcasted_iota(jnp.int32, (CHUNK, STATE), 0)
    near = c_ref[...].astype(F32)
    for r in range(RESETS):
        scores = jnp.where((source < resets[r]) & (resets[r] <= target), 0.0, scores)
        near = jnp.where((resets[r] >= first) & (row >= resets[r]), 0.0, near)
    scores = scores.astype(BF16)
    near = near.astype(BF16)
    c = c_ref[...]
    for pair in range(PAIRS):
        rows = slice(pair * WIDE, (pair + 1) * WIDE)
        x = x_ref[:, rows].T.astype(F32)
        scaled = (x * pair_rows(before, pair)).astype(BF16)
        inside = dot(scaled, scores) + dot_nt(start_ref[0, rows, :], near)
        y = inside * pair_rows(after, pair)
        y = y + dot_nt(got_ref[rows, :], c) * pair_rows(level, pair)
        direct = jnp.concatenate(
            [x[:HEAD_DIM] * skip[2 * pair], x[HEAD_DIM:] * skip[2 * pair + 1]], axis=0
        )
        y_ref[0, rows, :] = y + direct


def inner(chunk0, count, place, resets, skip, inputs, state_in, state_out, log, level_weight, far, starts, got, factor, y):
    at = lambda c: (c + chunk0, 0)
    along = lambda c: (0, c + chunk0)
    operands = [place, resets, skip, inputs, state_in, state_out, log, level_weight, far, starts, got, factor]
    in_specs = [
        SMEM,
        SMEM,
        SMEM,
        pl.BlockSpec((CHUNK, FEATURES), at),
        pl.BlockSpec((CHUNK, STATE), at),
        pl.BlockSpec((CHUNK, STATE), at),
        pl.BlockSpec((HEADS, CHUNK), along),
        pl.BlockSpec((2, HEADS, CHUNK), lambda c: (0, 0, c + chunk0)),
        pl.BlockSpec((HEADS, CHUNK), along),
        pl.BlockSpec((1, FEATURES, STATE), lambda c: (c + chunk0, 0, 0)),
        whole((FEATURES + SPAN_ROWS, STATE)),
        whole((HEADS, STATE)),
    ]
    aliases = {}
    if y is not None:
        aliases = {len(operands): 0}
        operands.append(y)
        in_specs.append(pl.BlockSpec(memory_space=pl.ANY))
    return pl.pallas_call(
        functools.partial(inner_kernel, chunk0),
        grid=(count,),
        in_specs=in_specs,
        out_specs=pl.BlockSpec((1, FEATURES, CHUNK), lambda c: (c + chunk0, 0, 0)),
        out_shape=jax.ShapeDtypeStruct((CHUNKS, FEATURES, CHUNK), F32),
        input_output_aliases=aliases,
        compiler_params=pltpu.CompilerParams(**PARAMS),
        cost_estimate=pl.CostEstimate(
            flops=count * 2 * CHUNK * FEATURES * 512, bytes_accessed=count * 2_000_000, transcendentals=0
        ),
        name="inner" + str(chunk0),
    )(*operands)


def level_kernel(levels, final, place, c_ref, weight_ref, far_ref, *rest):
    count = len(levels)
    mine, other, factors = rest[:count], rest[count : 2 * count], rest[2 * count : 3 * count]
    y_in = rest[3 * count]
    y_ref = rest[3 * count + 1]
    states = rest[-1]

    @pl.when(pl.program_id(0) == 0)
    def _():
        for n in range(count):
            a, b = mine[n][:HALF, :], other[n][:HALF, :]

            @pl.when(place[1] == 0)
            def _():
                states[n, :HALF, :] = a
                states[n, HALF:, :] = b

            @pl.when(place[1] == 1)
            def _():
                states[n, :HALF, :] = b
                states[n, HALF:, :] = a

    far = far_ref[...]
    coefs = [weight_ref[levels[n]] * far * factors[n][:, 0:1] for n in range(count)]
    c = c_ref[...]
    squares = jnp.zeros((8, CHUNK), F32)
    for pair in range(PAIRS):
        rows = slice(pair * WIDE, (pair + 1) * WIDE)
        y = y_in[0, rows, :]
        for n in range(count):
            y = y + dot_nt(states[n, rows, :], c) * pair_rows(coefs[n], pair)
        y_ref[0, rows, :] = y
        if final:
            part = y * y
            for k in range(WIDE // 8):
                squares = squares + part[8 * k : 8 * k + 8]
    if final:
        rest[3 * count + 2][0] = jnp.sum(squares, axis=0, keepdims=True)


def add_levels(levels, final, place, state_out, level_weight, far, mine, other, factors, y):
    count = len(levels)
    along = lambda c: (0, c)
    block = pl.BlockSpec((1, FEATURES, CHUNK), lambda c: (c, 0, 0))
    out_specs = [block]
    out_shape = [jax.ShapeDtypeStruct((CHUNKS, FEATURES, CHUNK), F32)]
    if final:
        out_specs.append(pl.BlockSpec((1, 1, CHUNK), lambda c: (c, 0, 0)))
        out_shape.append(jax.ShapeDtypeStruct((CHUNKS, 1, CHUNK), F32))
    return pl.pallas_call(
        functools.partial(level_kernel, levels, final),
        grid=(CHUNKS,),
        in_specs=[
            SMEM,
            pl.BlockSpec((CHUNK, STATE), lambda c: (c, 0)),
            pl.BlockSpec((LEVELS, HEADS, CHUNK), lambda c: (0, 0, c)),
            pl.BlockSpec((HEADS, CHUNK), along),
        ]
        + [whole((HALF + SPAN_ROWS, STATE))] * (2 * count)
        + [whole((HEADS, STATE))] * count
        + [block],
        out_specs=out_specs,
        out_shape=out_shape,
        input_output_aliases={4 + 3 * count: 0},
        scratch_shapes=[pltpu.VMEM((count, FEATURES, STATE), BF16)],
        compiler_params=pltpu.CompilerParams(**PARAMS),
        cost_estimate=pl.CostEstimate(
            flops=count * 2 * TOK_DEV * FEATURES * STATE * 2, bytes_accessed=18_000_000, transcendentals=0
        ),
        name="levels" + str(levels[0]),
    )(place, state_out, level_weight, far, *mine, *other, *factors, y)


def norm_kernel(y_ref, s0, s1, s2, s3, gain_ref, out_ref):
    squares = (s0[0] + s1[0]) + (s2[0] + s3[0])
    scale = lax.rsqrt(squares * (1.0 / (HEAD_TOTAL * HEAD_DIM)) + EPSILON)
    for pair in range(PAIRS):
        rows = slice(pair * WIDE, (pair + 1) * WIDE)
        gain = gain_ref[rows, :]
        y = y_ref[0, rows, :] * scale * jnp.concatenate([gain, gain], axis=1)
        out_ref[:, rows] = y.astype(BF16).T


def normalize(y, squares, gain):
    part = pl.BlockSpec((1, 1, CHUNK), lambda c: (c, 0, 0))
    return pl.pallas_call(
        norm_kernel,
        grid=(CHUNKS,),
        in_specs=[pl.BlockSpec((1, FEATURES, CHUNK), lambda c: (c, 0, 0))]
        + [part] * 4
        + [whole((FEATURES, STATE))],
        out_specs=pl.BlockSpec((CHUNK, FEATURES), lambda c: (c, 0)),
        out_shape=jax.ShapeDtypeStruct((TOK_DEV, FEATURES), BF16),
        compiler_params=pltpu.CompilerParams(**PARAMS),
        name="normalize",
    )(y, *squares, gain)


def swap(array, axis, distance, only_up=None):
    count = lax.axis_size(axis)
    route = [
        (low, low ^ distance)
        for low in range(count)
        if only_up is None or not low >> only_up & 1
    ]
    return lax.ppermute(array, axis, route)


def per_device(inputs, state_in, state_out, log_decay, level_weight, skip, norm_gain, resets):
    index = lax.axis_index("seq").astype(jnp.int32)
    place = jnp.stack([index, index & 1] + [index >> bit & 1 for bit in range(6)])
    gain = jnp.broadcast_to(norm_gain[:, None], (FEATURES, STATE))
    total, pay, starts, log, far, span = block_states(place, resets, inputs, state_in, log_decay)
    lead = jnp.ones((HEADS, STATE), F32)
    got = swap(pay, "seq", 1)
    one = got
    group, span, lead, one_factor, pay = join(0, True, place, total, span, lead, got)
    mine, other, factors = [], [], []
    for distance, bit in STEPS:
        got = swap(pay, "seq", distance, bit if bit == 5 else None)
        mine.append(got)
        other.append(swap(got, "seq", 1))
        if bit < 5:
            group, span, lead, factor, pay = join(bit, False, place, group, span, lead, got)
            factors.append(factor)
        else:
            factors.append(jnp.where(index >> bit & 1 == 1, lead, 0.0))
    y = None
    for chunk in range(0, CHUNKS, PIECE):
        y = inner(
            chunk, PIECE, place, resets, skip, inputs, state_in, state_out, log, level_weight, far, starts, one, one_factor, y
        )
    (y,) = add_levels((2, 3, 4), False, place, state_out, level_weight, far, mine[:3], other[:3], factors[:3], y)
    y, squares = add_levels((5, 6), True, place, state_out, level_weight, far, mine[3:], other[3:], factors[3:], y)
    shares = [squares] + [
        lax.ppermute(squares, "head", [(i, i ^ d) for i in range(4)]) for d in (1, 3, 2)
    ]
    return normalize(y, shares, gain)


def solution(mesh):
    placed = (
        P("seq", "head"),
        P("seq", None),
        P("seq", None),
        P("head", "seq"),
        P(None, "head", "seq"),
        P("head"),
        P("head"),
        P(),
    )
    return jax.shard_map(
        per_device, mesh=mesh, in_specs=placed, out_specs=P("seq", "head"), check_vma=False
    )
```

```python
import functools

import jax
import jax.numpy as jnp
from jax import lax
from jax.experimental import pallas as pl
from jax.experimental.pallas import tpu as pltpu
from jax.sharding import PartitionSpec as P

HEAD_TOTAL = 64
HEAD_DIM = 64
STATE = 128
LEVELS = 7
TOK_DEV = 2048
EPSILON = 1e-05

CHUNK = 256
CHUNKS = TOK_DEV // CHUNK
HEADS = 16
FEATURES = HEADS * HEAD_DIM
HALF = FEATURES // 2
HALF_HEADS = HEADS // 2
GROUP_HEADS = 8
WIDE = GROUP_HEADS * HEAD_DIM
GROUPS = HEADS // GROUP_HEADS
SPAN_ROWS = HEADS
RESETS = 4
PIECE = 2

F32 = jnp.float32
BF16 = jnp.bfloat16
PARAMS = dict(vmem_limit_bytes=16 * 1024 * 1024)
SMEM = pl.BlockSpec(memory_space=pltpu.SMEM)
VMEM = pl.BlockSpec(memory_space=pltpu.VMEM)
ANY = pl.BlockSpec(memory_space=pl.ANY)


def side(bit):
    return lax.axis_index("seq") >> bit & 1


def in_hbm(array):
    return pltpu.with_memory_space_constraint(array, pltpu.HBM)


def dot(a, b):
    return lax.dot_general(a, b, (((1,), (0,)), ((), ())), preferred_element_type=F32)


def dot_nt(a, b):
    return lax.dot_general(a, b, (((1,), (1,)), ((), ())), preferred_element_type=F32)


def head_rows(values, group):
    width = values.shape[1]
    heads = range(group * GROUP_HEADS, (group + 1) * GROUP_HEADS)
    return jnp.concatenate(
        [jnp.broadcast_to(values[h : h + 1, :], (HEAD_DIM, width)) for h in heads], axis=0
    )


def head_column(values, group, width):
    heads = range(group * GROUP_HEADS, (group + 1) * GROUP_HEADS)
    return jnp.concatenate(
        [jnp.broadcast_to(values[h : h + 1, 0:1], (HEAD_DIM, width)) for h in heads], axis=0
    )


def write_spans(ref, first, span):
    high = span.astype(BF16).astype(F32)
    middle = (span - high).astype(BF16).astype(F32)
    low = span - high - middle
    lane = lax.broadcasted_iota(jnp.int32, span.shape, 1)
    parts = jnp.where(lane < 32, high, jnp.where(lane < 64, middle, low))
    ref[first : first + SPAN_ROWS, :] = parts.astype(BF16)


def read_spans(ref, first):
    parts = ref[first : first + SPAN_ROWS, :].astype(F32)
    span = parts[:, 0:1] + parts[:, 32:33] + parts[:, 64:65]
    return jnp.broadcast_to(span, (HEADS, STATE))


def state_kernel(listed, x_any, b_any, c_any, decay_any, weight_any, *rest):
    total_ref, pay_ref, start_ref, log_ref, far_ref, span_ref, x_ref, b_ref, c_ref, weight_ref = rest[:10]
    x_in, decay_ref, state, sems, x_sems = rest[10:]
    base = lax.axis_index("seq") * TOK_DEV
    resets = [listed[r] for r in range(RESETS)]
    decay_copy = pltpu.make_async_copy(decay_any, decay_ref, sems.at[0])
    b_copy = pltpu.make_async_copy(b_any, b_ref, sems.at[1])
    later = [
        pltpu.make_async_copy(c_any, c_ref, sems.at[2]),
        pltpu.make_async_copy(weight_any, weight_ref, sems.at[3]),
    ]
    x_copies = []
    for k in range(CHUNKS):
        rows = slice(k * CHUNK, (k + 1) * CHUNK)
        x_copies.append(pltpu.make_async_copy(x_any.at[rows, :], x_in.at[k], x_sems.at[k]))
    for copy in [decay_copy, b_copy] + x_copies + later:
        copy.start()
    state[...] = jnp.zeros_like(state)
    square = (CHUNK, CHUNK)
    upto = lax.broadcasted_iota(jnp.int32, square, 0) <= lax.broadcasted_iota(
        jnp.int32, square, 1
    )
    ones = upto.astype(F32).astype(BF16)
    decay_copy.wait()
    rows = jnp.concatenate(
        [decay_ref[:, k * CHUNK : (k + 1) * CHUNK] for k in range(CHUNKS)], axis=0
    )
    high = rows.astype(BF16)
    rest_of = rows - high.astype(F32)
    middle = rest_of.astype(BF16)
    low = (rest_of - middle.astype(F32)).astype(BF16)
    sums = dot(high, ones) + dot(middle, ones) + dot(low, ones)
    before = jnp.zeros((HEADS, 1), F32)
    b_copy.wait()
    for k in range(CHUNKS):
        log = sums[k * HEADS : (k + 1) * HEADS]
        lanes = slice(k * CHUNK, (k + 1) * CHUNK)
        end = log[:, CHUNK - 1 : CHUNK]
        first = base + k * CHUNK
        last = first + CHUNK - 1
        position = first + lax.broadcasted_iota(jnp.int32, (HEADS, CHUNK), 1)
        weight = jnp.exp(end - log)
        kept = jnp.exp(end)
        far = jnp.exp(before + log)
        for reset in resets:
            weight = jnp.where((position < reset) & (reset <= last), 0.0, weight)
            kept = jnp.where((reset >= first) & (reset <= last), 0.0, kept)
            far = jnp.where((reset >= base) & (position >= reset), 0.0, far)
        log_ref[:, lanes] = log
        far_ref[:, lanes] = far
        before = before + end
        if k == CHUNKS - 1:
            span_ref[...] = jnp.broadcast_to(far[:, CHUNK - 1 : CHUNK], (HEADS, STATE))
        middle = jnp.exp(0.5 * end)
        b = b_ref[lanes, :]
        x_copies[k].wait()
        for group in range(GROUPS):
            rows = slice(group * WIDE, (group + 1) * WIDE)
            held = state[rows, :]
            start_ref[k, rows, :] = (held * head_column(middle, group, STATE)).astype(BF16)
            x = x_in[k, :, rows].T
            x_ref[k, rows, :] = x
            scaled = (x.astype(F32) * head_rows(weight, group)).astype(BF16)
            state[rows, :] = held * head_column(kept, group, STATE) + dot(scaled, b)
    total = state[...]
    total_ref[...] = total
    pay_ref[:FEATURES, :] = total.astype(BF16)
    write_spans(pay_ref, FEATURES, span_ref[...])
    for copy in later:
        copy.wait()


def block_states(resets, inputs, state_in, state_out, log_decay, level_weight):
    return pl.pallas_call(
        state_kernel,
        in_specs=[SMEM] + [ANY] * 5,
        out_specs=[VMEM] * 10,
        out_shape=[
            jax.ShapeDtypeStruct((FEATURES, STATE), F32),
            jax.ShapeDtypeStruct((FEATURES + SPAN_ROWS, STATE), BF16),
            jax.ShapeDtypeStruct((CHUNKS, FEATURES, STATE), BF16),
            jax.ShapeDtypeStruct((HEADS, TOK_DEV), F32),
            jax.ShapeDtypeStruct((HEADS, TOK_DEV), F32),
            jax.ShapeDtypeStruct((HEADS, STATE), F32),
            jax.ShapeDtypeStruct((CHUNKS, FEATURES, CHUNK), BF16),
            jax.ShapeDtypeStruct((TOK_DEV, STATE), BF16),
            jax.ShapeDtypeStruct((TOK_DEV, STATE), BF16),
            jax.ShapeDtypeStruct((LEVELS, HEADS, TOK_DEV), F32),
        ],
        scratch_shapes=[
            pltpu.VMEM((CHUNKS, CHUNK, FEATURES), BF16),
            pltpu.VMEM((HEADS, TOK_DEV), F32),
            pltpu.VMEM((FEATURES, STATE), F32),
            pltpu.SemaphoreType.DMA((4,)),
            pltpu.SemaphoreType.DMA((CHUNKS,)),
        ],
        compiler_params=pltpu.CompilerParams(**PARAMS),
        name="block_states",
    )(
        in_hbm(resets),
        in_hbm(inputs),
        in_hbm(state_in),
        in_hbm(state_out),
        in_hbm(log_decay),
        in_hbm(level_weight),
    )


def own_heads(span):
    return jnp.where(side(0) == 0, span[:HALF_HEADS], span[HALF_HEADS:])


def join_kernel(bit, own_ref, span_ref, *rest):
    *lead_ref, got_ref = rest[:-5]
    sum_ref, new_span_ref, new_lead_ref, factor_ref, pay_ref = rest[-5:]
    upper = side(bit) == 1
    first = bit == 0
    span = span_ref[...]
    lead = jnp.ones_like(span) if first else lead_ref[0][...]
    got_span = read_spans(got_ref, FEATURES if first else HALF)
    factor_ref[...] = jnp.where(upper, lead, 0.0)
    new_lead_ref[...] = jnp.where(upper, lead * got_span, lead)
    both = span * got_span
    new_span_ref[...] = both
    own_factor = jnp.where(upper, 1.0, own_heads(got_span))
    got_factor = jnp.where(upper, own_heads(span), 1.0)
    offset = side(0) * HALF if first else 0
    for h in range(HALF_HEADS):
        rows = pl.ds(pl.multiple_of(offset + h * HEAD_DIM, HEAD_DIM), HEAD_DIM)
        got = got_ref[rows, :].astype(F32)
        new = own_ref[rows, :] * own_factor[h : h + 1] + got * got_factor[h : h + 1]
        here = slice(h * HEAD_DIM, (h + 1) * HEAD_DIM)
        sum_ref[here, :] = new
        pay_ref[here, :] = new.astype(BF16)
    write_spans(pay_ref, HALF, both)


SMALL = jax.ShapeDtypeStruct((HEADS, STATE), F32)
HALF_SUM = jax.ShapeDtypeStruct((HALF, STATE), F32)
HALF_PAY = jax.ShapeDtypeStruct((HALF + SPAN_ROWS, STATE), BF16)


def join(bit, *operands):
    return pl.pallas_call(
        functools.partial(join_kernel, bit),
        in_specs=[VMEM] * len(operands),
        out_specs=[VMEM] * 5,
        out_shape=[HALF_SUM, SMALL, SMALL, SMALL, HALF_PAY],
        compiler_params=pltpu.CompilerParams(**PARAMS),
        name="join" + str(bit),
    )(*operands)


def join_chips_kernel(own_ref, span_ref, lead_ref, one_ref, two_ref, three_ref, *rest):
    sum_ref, new_span_ref, new_lead_ref, low_ref, high_ref, pay_ref, states_ref = rest[-7:]
    low_upper = side(1) == 1
    high_upper = side(2) == 1
    span, lead = span_ref[...], lead_ref[...]
    one, two, three = (read_spans(ref, HALF) for ref in (one_ref, two_ref, three_ref))
    low_ref[...] = jnp.where(low_upper, lead, 0.0)
    lead = jnp.where(low_upper, lead * one, lead)
    high_ref[...] = jnp.where(high_upper, lead, 0.0)
    near, away = span * one, two * three
    new_lead_ref[...] = jnp.where(high_upper, lead * away, lead)
    both = near * away
    new_span_ref[...] = both
    own_here = jnp.where(low_upper, 1.0, own_heads(one))
    one_here = jnp.where(low_upper, own_heads(span), 1.0)
    two_here = jnp.where(low_upper, 1.0, own_heads(three))
    three_here = jnp.where(low_upper, own_heads(two), 1.0)
    near_here = jnp.where(high_upper, 1.0, own_heads(away))
    away_here = jnp.where(high_upper, own_heads(near), 1.0)
    for h in range(HALF_HEADS):
        here = slice(h * HEAD_DIM, (h + 1) * HEAD_DIM)
        row = slice(h, h + 1)
        got = one_ref[here, :]
        here_sum = own_ref[here, :] * own_here[row] + got.astype(F32) * one_here[row]
        away_sum = two_ref[here, :].astype(F32) * two_here[row] + three_ref[here, :].astype(
            F32
        ) * three_here[row]
        new = here_sum * near_here[row] + away_sum * away_here[row]
        sum_ref[here, :] = new
        pay_ref[here, :] = new.astype(BF16)
        states_ref[here, :] = got
        states_ref[HALF + h * HEAD_DIM : HALF + (h + 1) * HEAD_DIM, :] = away_sum.astype(BF16)
    write_spans(pay_ref, HALF, both)


def join_chips(own, span, lead, got):
    return pl.pallas_call(
        join_chips_kernel,
        in_specs=[VMEM] * 6,
        out_specs=[VMEM] * 7,
        out_shape=[
            HALF_SUM,
            SMALL,
            SMALL,
            SMALL,
            SMALL,
            HALF_PAY,
            jax.ShapeDtypeStruct((FEATURES, STATE), BF16),
        ],
        compiler_params=pltpu.CompilerParams(**PARAMS),
        name="join_chips",
    )(own, span, lead, *got)


LATER = LEVELS - 2


def inner_kernel(chunks, listed, skip, x_ref, b_ref, c_ref, log_ref, weight_ref, far_ref, start_ref, got_ref, factor_ref, *rest):
    y_ref, flipped_ref, coef_ref = rest[-3:]
    square = (CHUNK, CHUNK)
    for chunk in chunks:
        first = lax.axis_index("seq") * TOK_DEV + chunk * CHUNK
        lanes = slice(chunk * CHUNK, (chunk + 1) * CHUNK)
        log = log_ref[:, lanes]
        far = far_ref[:, lanes]
        middle = 0.5 * log[:, CHUNK - 1 : CHUNK]
        after = weight_ref[0, :, lanes] * jnp.exp(log - middle)
        before = jnp.exp(middle - log)
        level = weight_ref[1, :, lanes] * far * factor_ref[:, 0:1]
        for n in range(LATER):
            coef_ref[n, :, lanes] = weight_ref[2 + n, :, lanes] * far
        source = first + lax.broadcasted_iota(jnp.int32, square, 0)
        target = first + lax.broadcasted_iota(jnp.int32, square, 1)
        c = c_ref[lanes, :].T
        flipped_ref[:, lanes] = c
        scores = dot(b_ref[lanes, :], c)
        scores = jnp.where(source <= target, scores, 0.0)
        reached = first + lax.broadcasted_iota(jnp.int32, (STATE, CHUNK), 1)
        near = c.astype(F32)
        for r in range(RESETS):
            reset = listed[r]
            scores = jnp.where((source < reset) & (reset <= target), 0.0, scores)
            near = jnp.where((reset >= first) & (reached >= reset), 0.0, near)
        scores = scores.astype(BF16)
        near = near.astype(BF16)
        for group in range(GROUPS):
            rows = slice(group * WIDE, (group + 1) * WIDE)
            x = x_ref[chunk, rows, :].astype(F32)
            scaled = (x * head_rows(before, group)).astype(BF16)
            inside = dot(scaled, scores) + dot(start_ref[chunk, rows, :], near)
            y = inside * head_rows(after, group)
            y = y + dot(got_ref[rows, :], c) * head_rows(level, group)
            direct = jnp.concatenate(
                [
                    x[h * HEAD_DIM : (h + 1) * HEAD_DIM] * skip[group * GROUP_HEADS + h]
                    for h in range(GROUP_HEADS)
                ],
                axis=0,
            )
            y_ref[chunk, rows, :] = y + direct


def inner(chunk0, operands, parts):
    resets, skip, *others = operands
    operands = [in_hbm(resets), in_hbm(skip)] + others
    in_specs = [SMEM, SMEM] + [VMEM] * len(others)
    aliases = {}
    if parts is not None:
        aliases = {len(operands) + n: n for n in range(3)}
        operands += parts
        in_specs += [VMEM] * 3
    return list(
        pl.pallas_call(
            functools.partial(inner_kernel, range(chunk0, chunk0 + PIECE)),
            in_specs=in_specs,
            out_specs=[VMEM] * 3,
            out_shape=[
                jax.ShapeDtypeStruct((CHUNKS, FEATURES, CHUNK), F32),
                jax.ShapeDtypeStruct((STATE, TOK_DEV), BF16),
                jax.ShapeDtypeStruct((LATER, HEADS, TOK_DEV), F32),
            ],
            input_output_aliases=aliases,
            compiler_params=pltpu.CompilerParams(**PARAMS),
            cost_estimate=pl.CostEstimate(
                flops=PIECE * 2 * CHUNK * FEATURES * 768, bytes_accessed=PIECE * 2_000_000, transcendentals=0
            ),
            name="inner" + str(chunk0),
        )(*operands)
    )


def level_kernel(levels, parts, final, flipped_ref, coef_ref, *rest):
    count = len(levels)
    mine, other = rest[:parts], rest[parts : 2 * parts]
    factors = rest[2 * parts : 2 * parts + count]
    y_ref, states = rest[-2 - final], rest[-1]
    lower = side(0) == 0
    factors = [factor[:, 0:1] for factor in factors]
    if final:
        factors = [jnp.where(side(LEVELS - 2) == 1, factor, 0.0) for factor in factors]
    for n in range(count):
        part, start = (0, n * HALF) if parts == 1 else (n, 0)
        a = mine[part][start : start + HALF, :].astype(F32)
        b = other[part][start : start + HALF, :].astype(F32)
        states[n, :HALF, :] = jnp.where(lower, a, b).astype(BF16)
        states[n, HALF:, :] = jnp.where(lower, b, a).astype(BF16)
    for chunk in range(CHUNKS):
        lanes = slice(chunk * CHUNK, (chunk + 1) * CHUNK)
        coefs = [coef_ref[level - 2, :, lanes] * factors[n] for n, level in enumerate(levels)]
        c = flipped_ref[:, lanes]
        squares = jnp.zeros((8, CHUNK), F32)
        for group in range(GROUPS):
            rows = slice(group * WIDE, (group + 1) * WIDE)
            y = y_ref[chunk, rows, :]
            for n in range(count):
                y = y + dot(states[n, rows, :], c) * head_rows(coefs[n], group)
            y_ref[chunk, rows, :] = y
            if final:
                part = y * y
                for k in range(WIDE // 8):
                    squares = squares + part[8 * k : 8 * k + 8]
        if final:
            rest[-2][chunk] = jnp.sum(squares, axis=0, keepdims=True)


def add_levels(levels, final, mine, other, factors, y, flipped, coef):
    count = len(levels)
    operands = [flipped, coef, *mine, *other, *factors]
    return pl.pallas_call(
        functools.partial(level_kernel, levels, len(mine), final),
        in_specs=[VMEM] * (len(operands) + 1),
        out_specs=[VMEM] * (1 + final),
        out_shape=[
            jax.ShapeDtypeStruct((CHUNKS, FEATURES, CHUNK), F32),
            jax.ShapeDtypeStruct((CHUNKS, 1, CHUNK), F32),
        ][: 1 + final],
        input_output_aliases={len(operands): 0},
        scratch_shapes=[pltpu.VMEM((count, FEATURES, STATE), BF16)],
        compiler_params=pltpu.CompilerParams(**PARAMS),
        cost_estimate=pl.CostEstimate(
            flops=count * 4 * TOK_DEV * FEATURES * STATE, bytes_accessed=4_000_000, transcendentals=0
        ),
        name="levels" + str(levels[0]),
    )(*operands, y)


def flip_kernel(y_ref, gain_ref, out_ref):
    for chunk in range(CHUNKS):
        for group in range(GROUPS):
            rows = slice(group * WIDE, (group + 1) * WIDE)
            y = y_ref[chunk, rows, :].T
            out_ref[chunk * CHUNK : (chunk + 1) * CHUNK, rows] = y * gain_ref[:, rows]


def flip(y, gain):
    return pl.pallas_call(
        flip_kernel,
        in_specs=[VMEM] * 2,
        out_specs=VMEM,
        out_shape=jax.ShapeDtypeStruct((TOK_DEV, FEATURES), F32),
        compiler_params=pltpu.CompilerParams(**PARAMS),
        cost_estimate=pl.CostEstimate(flops=0, bytes_accessed=16_000_000, transcendentals=0),
        name="flip",
    )(y, gain)


def norm_kernel(y_ref, s0, s1, s2, s3, out_any, buffers, sems):
    copies = []
    for chunk in range(CHUNKS):
        rows = slice(chunk * CHUNK, (chunk + 1) * CHUNK)
        squares = (s0[chunk] + s1[chunk]) + (s2[chunk] + s3[chunk])
        scale = lax.rsqrt(squares * (1.0 / (HEAD_TOTAL * HEAD_DIM)) + EPSILON)
        scale = jnp.broadcast_to(scale, (STATE, CHUNK)).T
        for column in range(FEATURES // STATE):
            columns = slice(column * STATE, (column + 1) * STATE)
            buffers[rows, columns] = (y_ref[rows, columns] * scale).astype(BF16)
        copies.append(
            pltpu.make_async_copy(buffers.at[rows, :], out_any.at[rows, :], sems.at[chunk])
        )
        copies[chunk].start()
    for copy in copies:
        copy.wait()


def normalize(y, squares):
    return pl.pallas_call(
        norm_kernel,
        in_specs=[VMEM] * 5,
        out_specs=ANY,
        out_shape=jax.ShapeDtypeStruct((TOK_DEV, FEATURES), BF16),
        scratch_shapes=[
            pltpu.VMEM((TOK_DEV, FEATURES), BF16),
            pltpu.SemaphoreType.DMA((CHUNKS,)),
        ],
        compiler_params=pltpu.CompilerParams(**PARAMS),
        name="normalize",
    )(y, *squares)


def swap(array, axis, distance, only_up=None):
    count = lax.axis_size(axis)
    route = [
        (low, low ^ distance)
        for low in range(count)
        if only_up is None or not low >> only_up & 1
    ]
    return lax.ppermute(array, axis, route)


def per_device(inputs, state_in, state_out, log_decay, level_weight, skip, norm_gain, resets):
    total, pay, starts, log, far, span, x, b, c, weights = block_states(
        resets, inputs, state_in, state_out, log_decay, level_weight
    )
    one = swap(pay, "seq", 1)
    half, span, lead, one_factor, pay = join(0, total, span, one)
    within = (resets, skip, x, b, c, log, weights, far, starts, one, one_factor)
    got = [swap(pay, "seq", distance) for distance in (2, 6, 4)]
    parts = inner(0, within, None)
    parts = inner(2, within, parts)
    got, parts = lax.optimization_barrier((got, parts))
    half, span, lead, two_factor, three_factor, pay, mine = join_chips(
        half, span, lead, (got[0], got[2], got[1])
    )
    four = swap(pay, "seq", 8)
    other = swap(mine, "seq", 1)
    parts = inner(4, within, parts)
    parts = inner(6, within, parts)
    four, parts = lax.optimization_barrier((four, parts))
    half, span, lead, four_factor, pay = join(3, half, span, lead, four)
    four, pay = lax.optimization_barrier((four, pay))
    y, flipped, coef = parts
    five = swap(pay, "seq", 16)
    four_other = swap(four, "seq", 1)
    (y,) = add_levels((2, 3), False, [mine], [other], [two_factor, three_factor], y, flipped, coef)
    five, y = lax.optimization_barrier((five, y))
    half, span, lead, five_factor, pay = join(4, half, span, lead, five)
    five, pay = lax.optimization_barrier((five, pay))
    six = swap(pay, "seq", 48, 5)
    five_other = swap(five, "seq", 1)
    (y,) = add_levels(
        (4, 5),
        False,
        [four, five],
        [four_other, five_other],
        [four_factor, five_factor],
        y,
        flipped,
        coef,
    )
    six, y = lax.optimization_barrier((six, y))
    six_other = swap(six, "seq", 1)
    y, squares = add_levels((6,), True, [six], [six_other], [lead], y, flipped, coef)
    shares = [squares] + [
        lax.ppermute(squares, "head", [(i, i ^ d) for i in range(4)]) for d in (1, 3, 2)
    ]
    return normalize(flip(y, norm_gain.reshape(1, FEATURES)), shares)


def solution(mesh):
    placed = (
        P("seq", "head"),
        P("seq", None),
        P("seq", None),
        P("head", "seq"),
        P(None, "head", "seq"),
        P("head"),
        P("head"),
        P(),
    )
    return jax.shard_map(
        per_device, mesh=mesh, in_specs=placed, out_specs=P("seq", "head"), check_vma=False
    )
```

```python
import functools

import jax
import jax.numpy as jnp
from jax import lax
from jax.experimental import pallas as pl
from jax.experimental.pallas import tpu as pltpu
from jax.sharding import PartitionSpec as P

HEAD_TOTAL = 64
HEAD_DIM = 64
STATE = 128
LEVELS = 7
TOK_DEV = 2048
EPSILON = 1e-05

CHUNK = 256
CHUNKS = TOK_DEV // CHUNK
HEADS = 16
FEATURES = HEADS * HEAD_DIM
HALF = FEATURES // 2
HALF_HEADS = HEADS // 2
CHIPS = 2
SHARD = HALF // CHIPS
SHARD_HEADS = HALF_HEADS // CHIPS
GROUP_HEADS = 8
WIDE = GROUP_HEADS * HEAD_DIM
GROUPS = HEADS // GROUP_HEADS
SPAN_ROWS = HEADS
RESETS = 4
PIECE = 2

F32 = jnp.float32
BF16 = jnp.bfloat16
PARAMS = dict(vmem_limit_bytes=16 * 1024 * 1024)
SMEM = pl.BlockSpec(memory_space=pltpu.SMEM)
VMEM = pl.BlockSpec(memory_space=pltpu.VMEM)
ANY = pl.BlockSpec(memory_space=pl.ANY)


def side(bit):
    return lax.axis_index("seq") >> bit & 1


def in_hbm(array):
    return pltpu.with_memory_space_constraint(array, pltpu.HBM)


def dot(a, b):
    return lax.dot_general(a, b, (((1,), (0,)), ((), ())), preferred_element_type=F32)


def dot_nt(a, b):
    return lax.dot_general(a, b, (((1,), (1,)), ((), ())), preferred_element_type=F32)


def head_rows(values, group):
    width = values.shape[1]
    heads = range(group * GROUP_HEADS, (group + 1) * GROUP_HEADS)
    return jnp.concatenate(
        [jnp.broadcast_to(values[h : h + 1, :], (HEAD_DIM, width)) for h in heads], axis=0
    )


def head_column(values, group, width):
    heads = range(group * GROUP_HEADS, (group + 1) * GROUP_HEADS)
    return jnp.concatenate(
        [jnp.broadcast_to(values[h : h + 1, 0:1], (HEAD_DIM, width)) for h in heads], axis=0
    )


def write_spans(ref, first, span):
    high = span.astype(BF16).astype(F32)
    middle = (span - high).astype(BF16).astype(F32)
    low = span - high - middle
    lane = lax.broadcasted_iota(jnp.int32, span.shape, 1)
    parts = jnp.where(lane < 32, high, jnp.where(lane < 64, middle, low))
    ref[first : first + SPAN_ROWS, :] = parts.astype(BF16)


def read_spans(ref, first):
    parts = ref[first : first + SPAN_ROWS, :].astype(F32)
    span = parts[:, 0:1] + parts[:, 32:33] + parts[:, 64:65]
    return jnp.broadcast_to(span, (HEADS, STATE))


def state_kernel(listed, x_any, b_any, c_any, decay_any, weight_any, *rest):
    total_ref, pay_ref, start_ref, log_ref, far_ref, span_ref, x_ref, b_ref, c_ref, weight_ref = rest[:10]
    x_in, decay_ref, state, sems, x_sems = rest[10:]
    base = lax.axis_index("seq") * TOK_DEV
    resets = [listed[r] for r in range(RESETS)]
    decay_copy = pltpu.make_async_copy(decay_any, decay_ref, sems.at[0])
    b_copy = pltpu.make_async_copy(b_any, b_ref, sems.at[1])
    later = [
        pltpu.make_async_copy(c_any, c_ref, sems.at[2]),
        pltpu.make_async_copy(weight_any, weight_ref, sems.at[3]),
    ]
    x_copies = []
    for k in range(CHUNKS):
        rows = slice(k * CHUNK, (k + 1) * CHUNK)
        x_copies.append(pltpu.make_async_copy(x_any.at[rows, :], x_in.at[k], x_sems.at[k]))
    for copy in [decay_copy, b_copy] + x_copies + later:
        copy.start()
    state[...] = jnp.zeros_like(state)
    square = (CHUNK, CHUNK)
    upto = lax.broadcasted_iota(jnp.int32, square, 0) <= lax.broadcasted_iota(
        jnp.int32, square, 1
    )
    ones = upto.astype(F32).astype(BF16)
    decay_copy.wait()
    rows = jnp.concatenate(
        [decay_ref[:, k * CHUNK : (k + 1) * CHUNK] for k in range(CHUNKS)], axis=0
    )
    high = rows.astype(BF16)
    rest_of = rows - high.astype(F32)
    middle = rest_of.astype(BF16)
    low = (rest_of - middle.astype(F32)).astype(BF16)
    sums = dot(high, ones) + dot(middle, ones) + dot(low, ones)
    before = jnp.zeros((HEADS, 1), F32)
    b_copy.wait()
    for k in range(CHUNKS):
        log = sums[k * HEADS : (k + 1) * HEADS]
        lanes = slice(k * CHUNK, (k + 1) * CHUNK)
        end = log[:, CHUNK - 1 : CHUNK]
        first = base + k * CHUNK
        last = first + CHUNK - 1
        position = first + lax.broadcasted_iota(jnp.int32, (HEADS, CHUNK), 1)
        weight = jnp.exp(end - log)
        kept = jnp.exp(end)
        far = jnp.exp(before + log)
        for reset in resets:
            weight = jnp.where((position < reset) & (reset <= last), 0.0, weight)
            kept = jnp.where((reset >= first) & (reset <= last), 0.0, kept)
            far = jnp.where((reset >= base) & (position >= reset), 0.0, far)
        log_ref[:, lanes] = log
        far_ref[:, lanes] = far
        before = before + end
        if k == CHUNKS - 1:
            span_ref[...] = jnp.broadcast_to(far[:, CHUNK - 1 : CHUNK], (HEADS, STATE))
        middle = jnp.exp(0.5 * end)
        b = b_ref[lanes, :]
        x_copies[k].wait()
        for group in range(GROUPS):
            rows = slice(group * WIDE, (group + 1) * WIDE)
            held = state[rows, :]
            start_ref[k, rows, :] = (held * head_column(middle, group, STATE)).astype(BF16)
            x = x_in[k, :, rows].T
            x_ref[k, rows, :] = x
            scaled = (x.astype(F32) * head_rows(weight, group)).astype(BF16)
            state[rows, :] = held * head_column(kept, group, STATE) + dot(scaled, b)
    total = state[...]
    total_ref[...] = total
    pay_ref[:FEATURES, :] = total.astype(BF16)
    write_spans(pay_ref, FEATURES, span_ref[...])
    for copy in later:
        copy.wait()


def block_states(resets, inputs, state_in, state_out, log_decay, level_weight):
    return pl.pallas_call(
        state_kernel,
        in_specs=[SMEM] + [ANY] * 5,
        out_specs=[VMEM] * 10,
        out_shape=[
            jax.ShapeDtypeStruct((FEATURES, STATE), F32),
            jax.ShapeDtypeStruct((FEATURES + SPAN_ROWS, STATE), BF16),
            jax.ShapeDtypeStruct((CHUNKS, FEATURES, STATE), BF16),
            jax.ShapeDtypeStruct((HEADS, TOK_DEV), F32),
            jax.ShapeDtypeStruct((HEADS, TOK_DEV), F32),
            jax.ShapeDtypeStruct((HEADS, STATE), F32),
            jax.ShapeDtypeStruct((CHUNKS, FEATURES, CHUNK), BF16),
            jax.ShapeDtypeStruct((TOK_DEV, STATE), BF16),
            jax.ShapeDtypeStruct((TOK_DEV, STATE), BF16),
            jax.ShapeDtypeStruct((LEVELS, HEADS, TOK_DEV), F32),
        ],
        scratch_shapes=[
            pltpu.VMEM((CHUNKS, CHUNK, FEATURES), BF16),
            pltpu.VMEM((HEADS, TOK_DEV), F32),
            pltpu.VMEM((FEATURES, STATE), F32),
            pltpu.SemaphoreType.DMA((4,)),
            pltpu.SemaphoreType.DMA((CHUNKS,)),
        ],
        compiler_params=pltpu.CompilerParams(**PARAMS),
        name="block_states",
    )(
        in_hbm(resets),
        in_hbm(inputs),
        in_hbm(state_in),
        in_hbm(state_out),
        in_hbm(log_decay),
        in_hbm(level_weight),
    )


def own_heads(span):
    return jnp.where(side(0) == 0, span[:HALF_HEADS], span[HALF_HEADS:])


def chip():
    return side(1)


def shard_head(span, head):
    row = side(0) * HALF_HEADS + chip() * SHARD_HEADS + head
    here = lax.broadcasted_iota(jnp.int32, span.shape, 0) == row
    return jnp.sum(jnp.where(here, span, 0.0), axis=0, keepdims=True)


def join_cores_kernel(own_ref, span_ref, got_ref, sum_ref, new_span_ref, new_lead_ref, factor_ref, pay_ref):
    upper = side(0) == 1
    span = span_ref[...]
    got_span = read_spans(got_ref, FEATURES)
    factor_ref[...] = jnp.broadcast_to(jnp.where(upper, 1.0, 0.0), span.shape)
    new_lead_ref[...] = jnp.where(upper, got_span, 1.0)
    both = span * got_span
    new_span_ref[...] = both
    own_factor = jnp.where(upper, 1.0, own_heads(got_span))
    got_factor = jnp.where(upper, own_heads(span), 1.0)
    for h in range(HALF_HEADS):
        rows = pl.ds(pl.multiple_of(side(0) * HALF + h * HEAD_DIM, HEAD_DIM), HEAD_DIM)
        got = got_ref[rows, :].astype(F32)
        new = own_ref[rows, :] * own_factor[h : h + 1] + got * got_factor[h : h + 1]
        here = slice(h * HEAD_DIM, (h + 1) * HEAD_DIM)
        sum_ref[here, :] = new
        pay_ref[here, :] = new.astype(BF16)
    write_spans(pay_ref, HALF, both)


def join_kernel(bit, own_ref, span_ref, lead_ref, got_ref, *rest):
    *below, sum_ref, new_span_ref, new_lead_ref, factor_ref, pay_ref = rest[: 5 + len(rest) // 6]
    if below:
        rest[-1][:SHARD, :] = below[0][:SHARD, :]
        rest[-1][SHARD:, :] = got_ref[:SHARD, :]
    upper = side(bit) == 1
    span, lead = span_ref[...], lead_ref[...]
    got_span = read_spans(got_ref, SHARD)
    factor_ref[...] = jnp.where(upper, lead, 0.0)
    new_lead_ref[...] = jnp.where(upper, lead * got_span, lead)
    both = span * got_span
    new_span_ref[...] = both
    for h in range(SHARD_HEADS):
        here = slice(h * HEAD_DIM, (h + 1) * HEAD_DIM)
        own_factor = jnp.where(upper, 1.0, shard_head(got_span, h))
        got_factor = jnp.where(upper, shard_head(span, h), 1.0)
        new = own_ref[here, :] * own_factor + got_ref[here, :].astype(F32) * got_factor
        sum_ref[here, :] = new
        pay_ref[here, :] = new.astype(BF16)
    write_spans(pay_ref, SHARD, both)


SMALL = jax.ShapeDtypeStruct((HEADS, STATE), F32)
HALF_SUM = jax.ShapeDtypeStruct((HALF, STATE), F32)
HALF_PAY = jax.ShapeDtypeStruct((HALF + SPAN_ROWS, STATE), BF16)
SHARD_SUM = jax.ShapeDtypeStruct((SHARD, STATE), F32)
SHARD_PAIR = jax.ShapeDtypeStruct((2 * SHARD, STATE), BF16)
SHARD_PAY = jax.ShapeDtypeStruct((SHARD + SPAN_ROWS, STATE), BF16)


def join_cores(*operands):
    return pl.pallas_call(
        join_cores_kernel,
        in_specs=[VMEM] * len(operands),
        out_specs=[VMEM] * 5,
        out_shape=[HALF_SUM, SMALL, SMALL, SMALL, HALF_PAY],
        compiler_params=pltpu.CompilerParams(**PARAMS),
        name="join_cores",
    )(*operands)


def join(bit, *operands):
    return pl.pallas_call(
        functools.partial(join_kernel, bit),
        in_specs=[VMEM] * len(operands),
        out_specs=[VMEM] * (5 + len(operands) // 5),
        out_shape=[SHARD_SUM, SMALL, SMALL, SMALL, SHARD_PAY, SHARD_PAIR][: 5 + len(operands) // 5],
        compiler_params=pltpu.CompilerParams(**PARAMS),
        name="join" + str(bit),
    )(*operands)


def gather_kernel(parts, *refs):
    out_ref = refs[-1]
    for distance in range(CHIPS):
        row = (chip() ^ distance) * SHARD
        for n in range(parts):
            rows = pl.ds(pl.multiple_of(row + n * HALF, SHARD), SHARD)
            out_ref[rows, :] = refs[distance][n * SHARD : (n + 1) * SHARD, :]


def gather(parts, own, got):
    return pl.pallas_call(
        functools.partial(gather_kernel, parts),
        in_specs=[VMEM] * CHIPS,
        out_specs=VMEM,
        out_shape=jax.ShapeDtypeStruct((parts * HALF, STATE), BF16),
        compiler_params=pltpu.CompilerParams(**PARAMS),
        name="gather" + str(parts),
    )(own, *got)


def join_chips_kernel(own_ref, span_ref, lead_ref, one_ref, two_ref, three_ref, *rest):
    sum_ref, new_span_ref, new_lead_ref, low_ref, high_ref, pay_ref, states_ref, sums = rest
    low_upper = side(1) == 1
    high_upper = side(2) == 1
    span, lead = span_ref[...], lead_ref[...]
    one, two, three = (read_spans(ref, HALF) for ref in (one_ref, two_ref, three_ref))
    low_ref[...] = jnp.where(low_upper, lead, 0.0)
    lead = jnp.where(low_upper, lead * one, lead)
    high_ref[...] = jnp.where(high_upper, lead, 0.0)
    near, away = span * one, two * three
    new_lead_ref[...] = jnp.where(high_upper, lead * away, lead)
    both = near * away
    new_span_ref[...] = both
    own_here = jnp.where(low_upper, 1.0, own_heads(one))
    one_here = jnp.where(low_upper, own_heads(span), 1.0)
    two_here = jnp.where(low_upper, 1.0, own_heads(three))
    three_here = jnp.where(low_upper, own_heads(two), 1.0)
    near_here = jnp.where(high_upper, 1.0, own_heads(away))
    away_here = jnp.where(high_upper, own_heads(near), 1.0)
    for h in range(HALF_HEADS):
        here = slice(h * HEAD_DIM, (h + 1) * HEAD_DIM)
        row = slice(h, h + 1)
        got = one_ref[here, :]
        here_sum = own_ref[here, :] * own_here[row] + got.astype(F32) * one_here[row]
        away_sum = two_ref[here, :].astype(F32) * two_here[row] + three_ref[here, :].astype(
            F32
        ) * three_here[row]
        new = here_sum * near_here[row] + away_sum * away_here[row]
        sums[here, :] = new
        states_ref[here, :] = got
        states_ref[HALF + h * HEAD_DIM : HALF + (h + 1) * HEAD_DIM, :] = away_sum.astype(BF16)
    shard = sums[pl.ds(pl.multiple_of(chip() * SHARD, SHARD), SHARD), :]
    sum_ref[...] = shard
    pay_ref[:SHARD, :] = shard.astype(BF16)
    write_spans(pay_ref, SHARD, both)


def join_chips(own, span, lead, got):
    return pl.pallas_call(
        join_chips_kernel,
        in_specs=[VMEM] * 6,
        out_specs=[VMEM] * 7,
        out_shape=[
            SHARD_SUM,
            SMALL,
            SMALL,
            SMALL,
            SMALL,
            SHARD_PAY,
            jax.ShapeDtypeStruct((FEATURES, STATE), BF16),
        ],
        scratch_shapes=[pltpu.VMEM((HALF, STATE), F32)],
        compiler_params=pltpu.CompilerParams(**PARAMS),
        name="join_chips",
    )(own, span, lead, *got)


LATER = LEVELS - 2


def inner_kernel(chunks, listed, skip, x_ref, b_ref, c_ref, log_ref, weight_ref, far_ref, start_ref, got_ref, factor_ref, *rest):
    y_ref, flipped_ref, coef_ref = rest[-3:]
    square = (CHUNK, CHUNK)
    for chunk in chunks:
        first = lax.axis_index("seq") * TOK_DEV + chunk * CHUNK
        lanes = slice(chunk * CHUNK, (chunk + 1) * CHUNK)
        log = log_ref[:, lanes]
        far = far_ref[:, lanes]
        middle = 0.5 * log[:, CHUNK - 1 : CHUNK]
        after = weight_ref[0, :, lanes] * jnp.exp(log - middle)
        before = jnp.exp(middle - log)
        level = weight_ref[1, :, lanes] * far * factor_ref[:, 0:1]
        for n in range(LATER):
            coef_ref[n, :, lanes] = weight_ref[2 + n, :, lanes] * far
        source = first + lax.broadcasted_iota(jnp.int32, square, 0)
        target = first + lax.broadcasted_iota(jnp.int32, square, 1)
        c = c_ref[lanes, :].T
        flipped_ref[:, lanes] = c
        scores = dot(b_ref[lanes, :], c)
        scores = jnp.where(source <= target, scores, 0.0)
        reached = first + lax.broadcasted_iota(jnp.int32, (STATE, CHUNK), 1)
        near = c.astype(F32)
        for r in range(RESETS):
            reset = listed[r]
            scores = jnp.where((source < reset) & (reset <= target), 0.0, scores)
            near = jnp.where((reset >= first) & (reached >= reset), 0.0, near)
        scores = scores.astype(BF16)
        near = near.astype(BF16)
        for group in range(GROUPS):
            rows = slice(group * WIDE, (group + 1) * WIDE)
            x = x_ref[chunk, rows, :].astype(F32)
            scaled = (x * head_rows(before, group)).astype(BF16)
            inside = dot(scaled, scores) + dot(start_ref[chunk, rows, :], near)
            y = inside * head_rows(after, group)
            y = y + dot(got_ref[rows, :], c) * head_rows(level, group)
            direct = jnp.concatenate(
                [
                    x[h * HEAD_DIM : (h + 1) * HEAD_DIM] * skip[group * GROUP_HEADS + h]
                    for h in range(GROUP_HEADS)
                ],
                axis=0,
            )
            y_ref[chunk, rows, :] = y + direct


def inner(chunk0, operands, parts):
    resets, skip, *others = operands
    operands = [in_hbm(resets), in_hbm(skip)] + others
    in_specs = [SMEM, SMEM] + [VMEM] * len(others)
    aliases = {}
    if parts is not None:
        aliases = {len(operands) + n: n for n in range(3)}
        operands += parts
        in_specs += [VMEM] * 3
    return list(
        pl.pallas_call(
            functools.partial(inner_kernel, range(chunk0, chunk0 + PIECE)),
            in_specs=in_specs,
            out_specs=[VMEM] * 3,
            out_shape=[
                jax.ShapeDtypeStruct((CHUNKS, FEATURES, CHUNK), F32),
                jax.ShapeDtypeStruct((STATE, TOK_DEV), BF16),
                jax.ShapeDtypeStruct((LATER, HEADS, TOK_DEV), F32),
            ],
            input_output_aliases=aliases,
            compiler_params=pltpu.CompilerParams(**PARAMS),
            cost_estimate=pl.CostEstimate(
                flops=PIECE * 2 * CHUNK * FEATURES * 768, bytes_accessed=PIECE * 2_000_000, transcendentals=0
            ),
            name="inner" + str(chunk0),
        )(*operands)
    )


def level_kernel(levels, parts, final, flipped_ref, coef_ref, *rest):
    count = len(levels)
    mine, other = rest[:parts], rest[parts : 2 * parts]
    factors = rest[2 * parts : 2 * parts + count]
    y_ref, states = rest[-2 - final], rest[-1]
    lower = side(0) == 0
    factors = [factor[:, 0:1] for factor in factors]
    if final:
        factors = [jnp.where(side(LEVELS - 2) == 1, factor, 0.0) for factor in factors]
    for n in range(count):
        part, start = (0, n * HALF) if parts == 1 else (n, 0)
        a = mine[part][start : start + HALF, :].astype(F32)
        b = other[part][start : start + HALF, :].astype(F32)
        states[n, :HALF, :] = jnp.where(lower, a, b).astype(BF16)
        states[n, HALF:, :] = jnp.where(lower, b, a).astype(BF16)
    for chunk in range(CHUNKS):
        lanes = slice(chunk * CHUNK, (chunk + 1) * CHUNK)
        coefs = [coef_ref[level - 2, :, lanes] * factors[n] for n, level in enumerate(levels)]
        c = flipped_ref[:, lanes]
        squares = jnp.zeros((8, CHUNK), F32)
        for group in range(GROUPS):
            rows = slice(group * WIDE, (group + 1) * WIDE)
            y = y_ref[chunk, rows, :]
            for n in range(count):
                y = y + dot(states[n, rows, :], c) * head_rows(coefs[n], group)
            y_ref[chunk, rows, :] = y
            if final:
                part = y * y
                for k in range(WIDE // 8):
                    squares = squares + part[8 * k : 8 * k + 8]
        if final:
            rest[-2][chunk] = jnp.sum(squares, axis=0, keepdims=True)


def add_levels(levels, final, mine, other, factors, y, flipped, coef):
    count = len(levels)
    operands = [flipped, coef, *mine, *other, *factors]
    return pl.pallas_call(
        functools.partial(level_kernel, levels, len(mine), final),
        in_specs=[VMEM] * (len(operands) + 1),
        out_specs=[VMEM] * (1 + final),
        out_shape=[
            jax.ShapeDtypeStruct((CHUNKS, FEATURES, CHUNK), F32),
            jax.ShapeDtypeStruct((CHUNKS, 1, CHUNK), F32),
        ][: 1 + final],
        input_output_aliases={len(operands): 0},
        scratch_shapes=[pltpu.VMEM((count, FEATURES, STATE), BF16)],
        compiler_params=pltpu.CompilerParams(**PARAMS),
        cost_estimate=pl.CostEstimate(
            flops=count * 4 * TOK_DEV * FEATURES * STATE, bytes_accessed=4_000_000, transcendentals=0
        ),
        name="levels" + str(levels[0]),
    )(*operands, y)


def flip_kernel(y_ref, gain_ref, out_ref):
    for chunk in range(CHUNKS):
        for group in range(GROUPS):
            rows = slice(group * WIDE, (group + 1) * WIDE)
            y = y_ref[chunk, rows, :].T
            out_ref[chunk * CHUNK : (chunk + 1) * CHUNK, rows] = y * gain_ref[:, rows]


def flip(y, gain):
    return pl.pallas_call(
        flip_kernel,
        in_specs=[VMEM] * 2,
        out_specs=VMEM,
        out_shape=jax.ShapeDtypeStruct((TOK_DEV, FEATURES), F32),
        compiler_params=pltpu.CompilerParams(**PARAMS),
        cost_estimate=pl.CostEstimate(flops=0, bytes_accessed=16_000_000, transcendentals=0),
        name="flip",
    )(y, gain)


def norm_kernel(y_ref, s0, s1, s2, s3, out_any, buffers, sems):
    copies = []
    for chunk in range(CHUNKS):
        rows = slice(chunk * CHUNK, (chunk + 1) * CHUNK)
        squares = (s0[chunk] + s1[chunk]) + (s2[chunk] + s3[chunk])
        scale = lax.rsqrt(squares * (1.0 / (HEAD_TOTAL * HEAD_DIM)) + EPSILON)
        scale = jnp.broadcast_to(scale, (STATE, CHUNK)).T
        for column in range(FEATURES // STATE):
            columns = slice(column * STATE, (column + 1) * STATE)
            buffers[rows, columns] = (y_ref[rows, columns] * scale).astype(BF16)
        copies.append(
            pltpu.make_async_copy(buffers.at[rows, :], out_any.at[rows, :], sems.at[chunk])
        )
        copies[chunk].start()
    for copy in copies:
        copy.wait()


def normalize(y, squares):
    return pl.pallas_call(
        norm_kernel,
        in_specs=[VMEM] * 5,
        out_specs=ANY,
        out_shape=jax.ShapeDtypeStruct((TOK_DEV, FEATURES), BF16),
        scratch_shapes=[
            pltpu.VMEM((TOK_DEV, FEATURES), BF16),
            pltpu.SemaphoreType.DMA((CHUNKS,)),
        ],
        compiler_params=pltpu.CompilerParams(**PARAMS),
        name="normalize",
    )(y, *squares)


def swap(array, axis, distance, only_up=None):
    count = lax.axis_size(axis)
    route = [
        (low, low ^ distance)
        for low in range(count)
        if only_up is None or not low >> only_up & 1
    ]
    return lax.ppermute(array, axis, route)


def per_device(inputs, state_in, state_out, log_decay, level_weight, skip, norm_gain, resets):
    total, pay, starts, log, far, span, x, b, c, weights = block_states(
        resets, inputs, state_in, state_out, log_decay, level_weight
    )
    one = swap(pay, "seq", 1)
    half, span, lead, one_factor, pay = join_cores(total, span, one)
    within = (resets, skip, x, b, c, log, weights, far, starts, one, one_factor)
    got = [swap(pay, "seq", distance) for distance in (2, 6, 4)]
    parts = inner(0, within, None)
    parts = inner(2, within, parts)
    got, parts = lax.optimization_barrier((got, parts))
    shard, span, lead, two_factor, three_factor, pay, mine = join_chips(
        half, span, lead, (got[0], got[2], got[1])
    )
    four = swap(pay, "seq", 8)
    mine, pay = lax.optimization_barrier((mine, pay))
    other = swap(mine, "seq", 1)
    parts = inner(4, within, parts)
    four, parts = lax.optimization_barrier((four, parts))
    shard, span, lead, four_factor, pay = join(3, shard, span, lead, four)
    five = swap(pay, "seq", 16)
    pay, parts = lax.optimization_barrier((pay, parts))
    parts = inner(6, within, parts)
    five, parts = lax.optimization_barrier((five, parts))
    y, flipped, coef = parts
    shard, span, lead, five_factor, pay, both = join(4, shard, span, lead, five, four)
    six = swap(pay, "seq", 48, 5)
    both, y = lax.optimization_barrier((both, y))
    both_got = swap(both, "seq", 2)
    (y,) = add_levels((2, 3), False, [mine], [other], [two_factor, three_factor], y, flipped, coef)
    both_got, six, y = lax.optimization_barrier((both_got, six, y))
    six_got = swap(six, "seq", 2)
    mine = gather(2, both, [both_got])
    other = swap(mine, "seq", 1)
    (y,) = add_levels((4, 5), False, [mine], [other], [four_factor, five_factor], y, flipped, coef)
    six_got, y = lax.optimization_barrier((six_got, y))
    mine = gather(1, six, [six_got])
    other = swap(mine, "seq", 1)
    y, squares = add_levels((6,), True, [mine], [other], [lead], y, flipped, coef)
    shares = [squares] + [
        lax.ppermute(squares, "head", [(i, i ^ d) for i in range(4)]) for d in (1, 3, 2)
    ]
    return normalize(flip(y, norm_gain.reshape(1, FEATURES)), shares)


def solution(mesh):
    placed = (
        P("seq", "head"),
        P("seq", None),
        P("seq", None),
        P("head", "seq"),
        P(None, "head", "seq"),
        P("head"),
        P("head"),
        P(),
    )
    return jax.shard_map(
        per_device, mesh=mesh, in_specs=placed, out_specs=P("seq", "head"), check_vma=False
    )
```

```python
import functools

import jax
import jax.numpy as jnp
from jax import lax
from jax.experimental import pallas as pl
from jax.experimental.pallas import tpu as pltpu
from jax.sharding import PartitionSpec as P

HEAD_TOTAL = 64
HEAD_DIM = 64
STATE = 128
LEVELS = 7
TOK_DEV = 2048
EPSILON = 1e-05

CHUNK = 256
CHUNKS = TOK_DEV // CHUNK
HEADS = 16
FEATURES = HEADS * HEAD_DIM
HALF = FEATURES // 2
HALF_HEADS = HEADS // 2
CHIPS = 2
SHARD = HALF // CHIPS
SHARD_HEADS = HALF_HEADS // CHIPS
GROUP_HEADS = 8
WIDE = GROUP_HEADS * HEAD_DIM
GROUPS = HEADS // GROUP_HEADS
SPAN_ROWS = HEADS
RESETS = 4
PIECE = 2

F32 = jnp.float32
BF16 = jnp.bfloat16
PARAMS = dict(vmem_limit_bytes=16 * 1024 * 1024)
SMEM = pl.BlockSpec(memory_space=pltpu.SMEM)
VMEM = pl.BlockSpec(memory_space=pltpu.VMEM)
ANY = pl.BlockSpec(memory_space=pl.ANY)


def side(bit):
    return lax.axis_index("seq") >> bit & 1


def in_hbm(array):
    return pltpu.with_memory_space_constraint(array, pltpu.HBM)


def dot(a, b):
    return lax.dot_general(a, b, (((1,), (0,)), ((), ())), preferred_element_type=F32)


def dot_nt(a, b):
    return lax.dot_general(a, b, (((1,), (1,)), ((), ())), preferred_element_type=F32)


def head_rows(values, group):
    width = values.shape[1]
    heads = range(group * GROUP_HEADS, (group + 1) * GROUP_HEADS)
    return jnp.concatenate(
        [jnp.broadcast_to(values[h : h + 1, :], (HEAD_DIM, width)) for h in heads], axis=0
    )


def head_column(values, group, width):
    heads = range(group * GROUP_HEADS, (group + 1) * GROUP_HEADS)
    return jnp.concatenate(
        [jnp.broadcast_to(values[h : h + 1, 0:1], (HEAD_DIM, width)) for h in heads], axis=0
    )


def write_spans(ref, first, span):
    high = span.astype(BF16).astype(F32)
    middle = (span - high).astype(BF16).astype(F32)
    low = span - high - middle
    lane = lax.broadcasted_iota(jnp.int32, span.shape, 1)
    parts = jnp.where(lane < 32, high, jnp.where(lane < 64, middle, low))
    ref[first : first + SPAN_ROWS, :] = parts.astype(BF16)


def read_spans(ref, first):
    parts = ref[first : first + SPAN_ROWS, :].astype(F32)
    span = parts[:, 0:1] + parts[:, 32:33] + parts[:, 64:65]
    return jnp.broadcast_to(span, (HEADS, STATE))


def state_kernel(listed, x_any, b_any, c_any, decay_any, weight_any, *rest):
    total_ref, pay_ref, start_ref, log_ref, far_ref, span_ref, x_ref, b_ref, c_ref, weight_ref = rest[:10]
    x_in, decay_ref, state, sems, x_sems = rest[10:]
    base = lax.axis_index("seq") * TOK_DEV
    resets = [listed[r] for r in range(RESETS)]
    decay_copy = pltpu.make_async_copy(decay_any, decay_ref, sems.at[0])
    b_copy = pltpu.make_async_copy(b_any, b_ref, sems.at[1])
    later = [
        pltpu.make_async_copy(c_any, c_ref, sems.at[2]),
        pltpu.make_async_copy(weight_any, weight_ref, sems.at[3]),
    ]
    x_copies = []
    for k in range(CHUNKS):
        rows = slice(k * CHUNK, (k + 1) * CHUNK)
        x_copies.append(pltpu.make_async_copy(x_any.at[rows, :], x_in.at[k], x_sems.at[k]))
    for copy in [decay_copy, b_copy] + x_copies + later:
        copy.start()
    state[...] = jnp.zeros_like(state)
    square = (CHUNK, CHUNK)
    upto = lax.broadcasted_iota(jnp.int32, square, 0) <= lax.broadcasted_iota(
        jnp.int32, square, 1
    )
    ones = upto.astype(F32).astype(BF16)
    decay_copy.wait()
    rows = jnp.concatenate(
        [decay_ref[:, k * CHUNK : (k + 1) * CHUNK] for k in range(CHUNKS)], axis=0
    )
    high = rows.astype(BF16)
    rest_of = rows - high.astype(F32)
    middle = rest_of.astype(BF16)
    low = (rest_of - middle.astype(F32)).astype(BF16)
    sums = dot(high, ones) + dot(middle, ones) + dot(low, ones)
    before = jnp.zeros((HEADS, 1), F32)
    b_copy.wait()
    for k in range(CHUNKS):
        log = sums[k * HEADS : (k + 1) * HEADS]
        lanes = slice(k * CHUNK, (k + 1) * CHUNK)
        end = log[:, CHUNK - 1 : CHUNK]
        first = base + k * CHUNK
        last = first + CHUNK - 1
        position = first + lax.broadcasted_iota(jnp.int32, (HEADS, CHUNK), 1)
        weight = jnp.exp(end - log)
        kept = jnp.exp(end)
        far = jnp.exp(before + log)
        for reset in resets:
            weight = jnp.where((position < reset) & (reset <= last), 0.0, weight)
            kept = jnp.where((reset >= first) & (reset <= last), 0.0, kept)
            far = jnp.where((reset >= base) & (position >= reset), 0.0, far)
        log_ref[:, lanes] = log
        far_ref[:, lanes] = far
        before = before + end
        if k == CHUNKS - 1:
            span_ref[...] = jnp.broadcast_to(far[:, CHUNK - 1 : CHUNK], (HEADS, STATE))
        middle = jnp.exp(0.5 * end)
        b = b_ref[lanes, :]
        x_copies[k].wait()
        for group in range(GROUPS):
            rows = slice(group * WIDE, (group + 1) * WIDE)
            held = state[rows, :]
            start_ref[k, rows, :] = (held * head_column(middle, group, STATE)).astype(BF16)
            x = x_in[k, :, rows].T
            x_ref[k, rows, :] = x
            scaled = (x.astype(F32) * head_rows(weight, group)).astype(BF16)
            state[rows, :] = held * head_column(kept, group, STATE) + dot(scaled, b)
    total = state[...]
    total_ref[...] = total
    pay_ref[:FEATURES, :] = total.astype(BF16)
    write_spans(pay_ref, FEATURES, span_ref[...])
    for copy in later:
        copy.wait()


def block_states(resets, inputs, state_in, state_out, log_decay, level_weight):
    return pl.pallas_call(
        state_kernel,
        in_specs=[SMEM] + [ANY] * 5,
        out_specs=[VMEM] * 10,
        out_shape=[
            jax.ShapeDtypeStruct((FEATURES, STATE), F32),
            jax.ShapeDtypeStruct((FEATURES + SPAN_ROWS, STATE), BF16),
            jax.ShapeDtypeStruct((CHUNKS, FEATURES, STATE), BF16),
            jax.ShapeDtypeStruct((HEADS, TOK_DEV), F32),
            jax.ShapeDtypeStruct((HEADS, TOK_DEV), F32),
            jax.ShapeDtypeStruct((HEADS, STATE), F32),
            jax.ShapeDtypeStruct((CHUNKS, FEATURES, CHUNK), BF16),
            jax.ShapeDtypeStruct((TOK_DEV, STATE), BF16),
            jax.ShapeDtypeStruct((TOK_DEV, STATE), BF16),
            jax.ShapeDtypeStruct((LEVELS, HEADS, TOK_DEV), F32),
        ],
        scratch_shapes=[
            pltpu.VMEM((CHUNKS, CHUNK, FEATURES), BF16),
            pltpu.VMEM((HEADS, TOK_DEV), F32),
            pltpu.VMEM((FEATURES, STATE), F32),
            pltpu.SemaphoreType.DMA((4,)),
            pltpu.SemaphoreType.DMA((CHUNKS,)),
        ],
        compiler_params=pltpu.CompilerParams(**PARAMS),
        name="block_states",
    )(
        in_hbm(resets),
        in_hbm(inputs),
        in_hbm(state_in),
        in_hbm(state_out),
        in_hbm(log_decay),
        in_hbm(level_weight),
    )


def own_heads(span):
    return jnp.where(side(0) == 0, span[:HALF_HEADS], span[HALF_HEADS:])


def chip():
    return side(1)


def shard_head(span, head):
    row = side(0) * HALF_HEADS + chip() * SHARD_HEADS + head
    here = lax.broadcasted_iota(jnp.int32, span.shape, 0) == row
    return jnp.sum(jnp.where(here, span, 0.0), axis=0, keepdims=True)


def join_cores_kernel(own_ref, span_ref, got_ref, sum_ref, new_span_ref, new_lead_ref, factor_ref, pay_ref):
    upper = side(0) == 1
    span = span_ref[...]
    got_span = read_spans(got_ref, FEATURES)
    factor_ref[...] = jnp.broadcast_to(jnp.where(upper, 1.0, 0.0), span.shape)
    new_lead_ref[...] = jnp.where(upper, got_span, 1.0)
    both = span * got_span
    new_span_ref[...] = both
    own_factor = jnp.where(upper, 1.0, own_heads(got_span))
    got_factor = jnp.where(upper, own_heads(span), 1.0)
    for h in range(HALF_HEADS):
        rows = pl.ds(pl.multiple_of(side(0) * HALF + h * HEAD_DIM, HEAD_DIM), HEAD_DIM)
        got = got_ref[rows, :].astype(F32)
        new = own_ref[rows, :] * own_factor[h : h + 1] + got * got_factor[h : h + 1]
        here = slice(h * HEAD_DIM, (h + 1) * HEAD_DIM)
        sum_ref[here, :] = new
        pay_ref[here, :] = new.astype(BF16)
    write_spans(pay_ref, HALF, both)


def join_kernel(bit, own_ref, span_ref, lead_ref, got_ref, *rest):
    last = bit == 4
    if last:
        below, both_ref = rest[0], rest[1]
        both_ref[:SHARD, :] = below[:SHARD, :]
        both_ref[SHARD:, :] = got_ref[:SHARD, :]
    new_lead_ref, factor_ref, pay_ref = rest[-3:]
    upper = side(bit) == 1
    span, lead = span_ref[...], lead_ref[...]
    got_span = read_spans(got_ref, SHARD)
    factor_ref[...] = jnp.where(upper, lead, 0.0)
    new_lead_ref[...] = jnp.where(upper, lead * got_span, lead)
    both = span * got_span
    if not last:
        rest[1][...] = both
    for h in range(SHARD_HEADS):
        here = slice(h * HEAD_DIM, (h + 1) * HEAD_DIM)
        own_factor = jnp.where(upper, 1.0, shard_head(got_span, h))
        got_factor = jnp.where(upper, shard_head(span, h), 1.0)
        new = own_ref[here, :] * own_factor + got_ref[here, :].astype(F32) * got_factor
        if not last:
            rest[0][here, :] = new
        pay_ref[here, :] = new.astype(BF16)
    write_spans(pay_ref, SHARD, both)


SMALL = jax.ShapeDtypeStruct((HEADS, STATE), F32)
HALF_SUM = jax.ShapeDtypeStruct((HALF, STATE), F32)
HALF_PAY = jax.ShapeDtypeStruct((HALF + SPAN_ROWS, STATE), BF16)
SHARD_SUM = jax.ShapeDtypeStruct((SHARD, STATE), F32)
SHARD_PAIR = jax.ShapeDtypeStruct((2 * SHARD, STATE), BF16)
SHARD_PAY = jax.ShapeDtypeStruct((SHARD + SPAN_ROWS, STATE), BF16)


def join_cores(*operands):
    return pl.pallas_call(
        join_cores_kernel,
        in_specs=[VMEM] * len(operands),
        out_specs=[VMEM] * 5,
        out_shape=[HALF_SUM, SMALL, SMALL, SMALL, HALF_PAY],
        compiler_params=pltpu.CompilerParams(**PARAMS),
        name="join_cores",
    )(*operands)


def join(bit, *operands):
    return pl.pallas_call(
        functools.partial(join_kernel, bit),
        in_specs=[VMEM] * len(operands),
        out_specs=[VMEM] * (4 if bit == 4 else 5),
        out_shape=([SHARD_PAIR] if bit == 4 else [SHARD_SUM, SMALL]) + [SMALL, SMALL, SHARD_PAY],
        compiler_params=pltpu.CompilerParams(**PARAMS),
        name="join" + str(bit),
    )(*operands)


def gather_kernel(parts, *refs):
    out_ref = refs[-1]
    for distance in range(CHIPS):
        row = (chip() ^ distance) * SHARD
        for n in range(parts):
            rows = pl.ds(pl.multiple_of(row + n * HALF, SHARD), SHARD)
            out_ref[rows, :] = refs[distance][n * SHARD : (n + 1) * SHARD, :]


def gather(parts, own, got):
    return pl.pallas_call(
        functools.partial(gather_kernel, parts),
        in_specs=[VMEM] * CHIPS,
        out_specs=VMEM,
        out_shape=jax.ShapeDtypeStruct((parts * HALF, STATE), BF16),
        compiler_params=pltpu.CompilerParams(**PARAMS),
        name="gather" + str(parts),
    )(own, *got)


def join_chips_kernel(own_ref, span_ref, lead_ref, one_ref, two_ref, three_ref, *rest):
    sum_ref, new_span_ref, new_lead_ref, low_ref, high_ref, pay_ref, states_ref, sums = rest
    low_upper = side(1) == 1
    high_upper = side(2) == 1
    span, lead = span_ref[...], lead_ref[...]
    one, two, three = (read_spans(ref, HALF) for ref in (one_ref, two_ref, three_ref))
    low_ref[...] = jnp.where(low_upper, lead, 0.0)
    lead = jnp.where(low_upper, lead * one, lead)
    high_ref[...] = jnp.where(high_upper, lead, 0.0)
    near, away = span * one, two * three
    new_lead_ref[...] = jnp.where(high_upper, lead * away, lead)
    both = near * away
    new_span_ref[...] = both
    own_here = jnp.where(low_upper, 1.0, own_heads(one))
    one_here = jnp.where(low_upper, own_heads(span), 1.0)
    two_here = jnp.where(low_upper, 1.0, own_heads(three))
    three_here = jnp.where(low_upper, own_heads(two), 1.0)
    near_here = jnp.where(high_upper, 1.0, own_heads(away))
    away_here = jnp.where(high_upper, own_heads(near), 1.0)
    for h in range(HALF_HEADS):
        here = slice(h * HEAD_DIM, (h + 1) * HEAD_DIM)
        row = slice(h, h + 1)
        got = one_ref[here, :]
        here_sum = own_ref[here, :] * own_here[row] + got.astype(F32) * one_here[row]
        away_sum = two_ref[here, :].astype(F32) * two_here[row] + three_ref[here, :].astype(
            F32
        ) * three_here[row]
        new = here_sum * near_here[row] + away_sum * away_here[row]
        sums[here, :] = new
        states_ref[here, :] = got
        states_ref[HALF + h * HEAD_DIM : HALF + (h + 1) * HEAD_DIM, :] = away_sum.astype(BF16)
    shard = sums[pl.ds(pl.multiple_of(chip() * SHARD, SHARD), SHARD), :]
    sum_ref[...] = shard
    pay_ref[:SHARD, :] = shard.astype(BF16)
    write_spans(pay_ref, SHARD, both)


def join_chips(own, span, lead, got):
    return pl.pallas_call(
        join_chips_kernel,
        in_specs=[VMEM] * 6,
        out_specs=[VMEM] * 7,
        out_shape=[
            SHARD_SUM,
            SMALL,
            SMALL,
            SMALL,
            SMALL,
            SHARD_PAY,
            jax.ShapeDtypeStruct((FEATURES, STATE), BF16),
        ],
        scratch_shapes=[pltpu.VMEM((HALF, STATE), F32)],
        compiler_params=pltpu.CompilerParams(**PARAMS),
        name="join_chips",
    )(own, span, lead, *got)


LATER = LEVELS - 2


def inner_kernel(chunks, listed, skip, x_ref, b_ref, c_ref, log_ref, weight_ref, far_ref, start_ref, got_ref, factor_ref, *rest):
    y_ref, flipped_ref, coef_ref = rest[-3:]
    square = (CHUNK, CHUNK)
    for chunk in chunks:
        first = lax.axis_index("seq") * TOK_DEV + chunk * CHUNK
        lanes = slice(chunk * CHUNK, (chunk + 1) * CHUNK)
        log = log_ref[:, lanes]
        far = far_ref[:, lanes]
        middle = 0.5 * log[:, CHUNK - 1 : CHUNK]
        after = weight_ref[0, :, lanes] * jnp.exp(log - middle)
        before = jnp.exp(middle - log)
        level = weight_ref[1, :, lanes] * far * factor_ref[:, 0:1]
        for n in range(LATER):
            coef_ref[n, :, lanes] = weight_ref[2 + n, :, lanes] * far
        source = first + lax.broadcasted_iota(jnp.int32, square, 0)
        target = first + lax.broadcasted_iota(jnp.int32, square, 1)
        c = c_ref[lanes, :].T
        flipped_ref[:, lanes] = c
        scores = dot(b_ref[lanes, :], c)
        scores = jnp.where(source <= target, scores, 0.0)
        reached = first + lax.broadcasted_iota(jnp.int32, (STATE, CHUNK), 1)
        near = c.astype(F32)
        for r in range(RESETS):
            reset = listed[r]
            scores = jnp.where((source < reset) & (reset <= target), 0.0, scores)
            near = jnp.where((reset >= first) & (reached >= reset), 0.0, near)
        scores = scores.astype(BF16)
        near = near.astype(BF16)
        for group in range(GROUPS):
            rows = slice(group * WIDE, (group + 1) * WIDE)
            x = x_ref[chunk, rows, :].astype(F32)
            scaled = (x * head_rows(before, group)).astype(BF16)
            inside = dot(scaled, scores) + dot(start_ref[chunk, rows, :], near)
            y = inside * head_rows(after, group)
            y = y + dot(got_ref[rows, :], c) * head_rows(level, group)
            direct = jnp.concatenate(
                [
                    x[h * HEAD_DIM : (h + 1) * HEAD_DIM] * skip[group * GROUP_HEADS + h]
                    for h in range(GROUP_HEADS)
                ],
                axis=0,
            )
            y_ref[chunk, rows, :] = y + direct


def inner(chunk0, operands, parts):
    resets, skip, *others = operands
    operands = [in_hbm(resets), in_hbm(skip)] + others
    in_specs = [SMEM, SMEM] + [VMEM] * len(others)
    aliases = {}
    if parts is not None:
        aliases = {len(operands) + n: n for n in range(3)}
        operands += parts
        in_specs += [VMEM] * 3
    return list(
        pl.pallas_call(
            functools.partial(inner_kernel, range(chunk0, chunk0 + PIECE)),
            in_specs=in_specs,
            out_specs=[VMEM] * 3,
            out_shape=[
                jax.ShapeDtypeStruct((CHUNKS, FEATURES, CHUNK), F32),
                jax.ShapeDtypeStruct((STATE, TOK_DEV), BF16),
                jax.ShapeDtypeStruct((LATER, HEADS, TOK_DEV), F32),
            ],
            input_output_aliases=aliases,
            compiler_params=pltpu.CompilerParams(**PARAMS),
            cost_estimate=pl.CostEstimate(
                flops=PIECE * 2 * CHUNK * FEATURES * 768, bytes_accessed=PIECE * 2_000_000, transcendentals=0
            ),
            name="inner" + str(chunk0),
        )(*operands)
    )


def level_kernel(levels, parts, final, flipped_ref, coef_ref, *rest):
    count = len(levels)
    mine, other = rest[:parts], rest[parts : 2 * parts]
    factors = rest[2 * parts : 2 * parts + count]
    y_ref, states = rest[-2 - final], rest[-1]
    lower = side(0) == 0
    factors = [factor[:, 0:1] for factor in factors]
    if final:
        factors = [jnp.where(side(LEVELS - 2) == 1, factor, 0.0) for factor in factors]
    for n in range(count):
        part, start = (0, n * HALF) if parts == 1 else (n, 0)
        a = mine[part][start : start + HALF, :].astype(F32)
        b = other[part][start : start + HALF, :].astype(F32)
        states[n, :HALF, :] = jnp.where(lower, a, b).astype(BF16)
        states[n, HALF:, :] = jnp.where(lower, b, a).astype(BF16)
    for chunk in range(CHUNKS):
        lanes = slice(chunk * CHUNK, (chunk + 1) * CHUNK)
        coefs = [coef_ref[level - 2, :, lanes] * factors[n] for n, level in enumerate(levels)]
        c = flipped_ref[:, lanes]
        squares = jnp.zeros((8, CHUNK), F32)
        for group in range(GROUPS):
            rows = slice(group * WIDE, (group + 1) * WIDE)
            y = y_ref[chunk, rows, :]
            for n in range(count):
                y = y + dot(states[n, rows, :], c) * head_rows(coefs[n], group)
            y_ref[chunk, rows, :] = y
            if final:
                part = y * y
                for k in range(WIDE // 8):
                    squares = squares + part[8 * k : 8 * k + 8]
        if final:
            rest[-2][chunk] = jnp.sum(squares, axis=0, keepdims=True)


def add_levels(levels, final, mine, other, factors, y, flipped, coef):
    count = len(levels)
    operands = [flipped, coef, *mine, *other, *factors]
    return pl.pallas_call(
        functools.partial(level_kernel, levels, len(mine), final),
        in_specs=[VMEM] * (len(operands) + 1),
        out_specs=[VMEM] * (1 + final),
        out_shape=[
            jax.ShapeDtypeStruct((CHUNKS, FEATURES, CHUNK), F32),
            jax.ShapeDtypeStruct((CHUNKS, 1, CHUNK), F32),
        ][: 1 + final],
        input_output_aliases={len(operands): 0},
        scratch_shapes=[pltpu.VMEM((count, FEATURES, STATE), BF16)],
        compiler_params=pltpu.CompilerParams(**PARAMS),
        cost_estimate=pl.CostEstimate(
            flops=count * 4 * TOK_DEV * FEATURES * STATE, bytes_accessed=4_000_000, transcendentals=0
        ),
        name="levels" + str(levels[0]),
    )(*operands, y)


def flip_kernel(y_ref, gain_ref, out_ref):
    for chunk in range(CHUNKS):
        for group in range(GROUPS):
            rows = slice(group * WIDE, (group + 1) * WIDE)
            y = y_ref[chunk, rows, :].T
            out_ref[chunk * CHUNK : (chunk + 1) * CHUNK, rows] = y * gain_ref[:, rows]


def flip(y, gain):
    return pl.pallas_call(
        flip_kernel,
        in_specs=[VMEM] * 2,
        out_specs=VMEM,
        out_shape=jax.ShapeDtypeStruct((TOK_DEV, FEATURES), F32),
        compiler_params=pltpu.CompilerParams(**PARAMS),
        cost_estimate=pl.CostEstimate(flops=0, bytes_accessed=16_000_000, transcendentals=0),
        name="flip",
    )(y, gain)


def norm_kernel(y_ref, s0, s1, s2, s3, out_any, buffers, sems):
    copies = []
    for chunk in range(CHUNKS):
        rows = slice(chunk * CHUNK, (chunk + 1) * CHUNK)
        squares = (s0[chunk] + s1[chunk]) + (s2[chunk] + s3[chunk])
        scale = lax.rsqrt(squares * (1.0 / (HEAD_TOTAL * HEAD_DIM)) + EPSILON)
        scale = jnp.broadcast_to(scale, (STATE, CHUNK)).T
        for column in range(FEATURES // STATE):
            columns = slice(column * STATE, (column + 1) * STATE)
            buffers[rows, columns] = (y_ref[rows, columns] * scale).astype(BF16)
        copies.append(
            pltpu.make_async_copy(buffers.at[rows, :], out_any.at[rows, :], sems.at[chunk])
        )
        copies[chunk].start()
    for copy in copies:
        copy.wait()


def normalize(y, squares):
    return pl.pallas_call(
        norm_kernel,
        in_specs=[VMEM] * 5,
        out_specs=ANY,
        out_shape=jax.ShapeDtypeStruct((TOK_DEV, FEATURES), BF16),
        scratch_shapes=[
            pltpu.VMEM((TOK_DEV, FEATURES), BF16),
            pltpu.SemaphoreType.DMA((CHUNKS,)),
        ],
        compiler_params=pltpu.CompilerParams(**PARAMS),
        name="normalize",
    )(y, *squares)


def swap(array, axis, distance, only_up=None):
    count = lax.axis_size(axis)
    route = [
        (low, low ^ distance)
        for low in range(count)
        if only_up is None or not low >> only_up & 1
    ]
    return lax.ppermute(array, axis, route)


def per_device(inputs, state_in, state_out, log_decay, level_weight, skip, norm_gain, resets):
    total, pay, starts, log, far, span, x, b, c, weights = block_states(
        resets, inputs, state_in, state_out, log_decay, level_weight
    )
    one = swap(pay, "seq", 1)
    half, span, lead, one_factor, pay = join_cores(total, span, one)
    within = (resets, skip, x, b, c, log, weights, far, starts, one, one_factor)
    got = [swap(pay, "seq", distance) for distance in (2, 6, 4)]
    parts = inner(0, within, None)
    parts = inner(2, within, parts)
    got, parts = lax.optimization_barrier((got, parts))
    shard, span, lead, two_factor, three_factor, pay, mine = join_chips(
        half, span, lead, (got[0], got[2], got[1])
    )
    four = swap(pay, "seq", 8)
    mine, pay = lax.optimization_barrier((mine, pay))
    other = swap(mine, "seq", 1)
    parts = inner(4, within, parts)
    four, parts = lax.optimization_barrier((four, parts))
    shard, span, lead, four_factor, pay = join(3, shard, span, lead, four)
    five = swap(pay, "seq", 16)
    pay, parts = lax.optimization_barrier((pay, parts))
    parts = inner(6, within, parts)
    five, parts = lax.optimization_barrier((five, parts))
    y, flipped, coef = parts
    both, lead, five_factor, pay = join(4, shard, span, lead, five, four)
    six = swap(pay, "seq", 48)
    both, y = lax.optimization_barrier((both, y))
    both_got = swap(both, "seq", 2)
    (y,) = add_levels((2, 3), False, [mine], [other], [two_factor, three_factor], y, flipped, coef)
    both_got, six, y = lax.optimization_barrier((both_got, six, y))
    six_got = swap(six, "seq", 2)
    mine = gather(2, both, [both_got])
    other = swap(mine, "seq", 1)
    (y,) = add_levels((4, 5), False, [mine], [other], [four_factor, five_factor], y, flipped, coef)
    six_got, y = lax.optimization_barrier((six_got, y))
    mine = gather(1, six, [six_got])
    other = swap(mine, "seq", 1)
    y, squares = add_levels((6,), True, [mine], [other], [lead], y, flipped, coef)
    shares = [squares] + [
        lax.ppermute(squares, "head", [(i, i ^ d) for i in range(4)]) for d in (1, 3, 2)
    ]
    return normalize(flip(y, norm_gain.reshape(1, FEATURES)), shares)


def solution(mesh):
    placed = (
        P("seq", "head"),
        P("seq", None),
        P("seq", None),
        P("head", "seq"),
        P(None, "head", "seq"),
        P("head"),
        P("head"),
        P(),
    )
    return jax.shard_map(
        per_device, mesh=mesh, in_specs=placed, out_specs=P("seq", "head"), check_vma=False
    )
```

```python
import functools

import jax
import jax.numpy as jnp
from jax import lax
from jax.experimental import pallas as pl
from jax.experimental.pallas import tpu as pltpu
from jax.sharding import PartitionSpec as P

HEAD_TOTAL = 64
HEAD_DIM = 64
STATE = 128
LEVELS = 7
TOK_DEV = 2048
EPSILON = 1e-05

CHUNK = 256
CHUNKS = TOK_DEV // CHUNK
HEADS = 16
FEATURES = HEADS * HEAD_DIM
HALF = FEATURES // 2
HALF_HEADS = HEADS // 2
CHIPS = 2
SHARD = HALF // CHIPS
SHARD_HEADS = HALF_HEADS // CHIPS
GROUP_HEADS = 8
AHEAD = 3
WIDE = GROUP_HEADS * HEAD_DIM
GROUPS = HEADS // GROUP_HEADS
SPAN_ROWS = HEADS
RESETS = 4
PIECE = 2

F32 = jnp.float32
BF16 = jnp.bfloat16
PARAMS = dict(vmem_limit_bytes=16 * 1024 * 1024)
SMEM = pl.BlockSpec(memory_space=pltpu.SMEM)
VMEM = pl.BlockSpec(memory_space=pltpu.VMEM)
ANY = pl.BlockSpec(memory_space=pl.ANY)


def side(bit):
    return lax.axis_index("seq") >> bit & 1


def in_hbm(array):
    return pltpu.with_memory_space_constraint(array, pltpu.HBM)


def dot(a, b):
    return lax.dot_general(a, b, (((1,), (0,)), ((), ())), preferred_element_type=F32)


def dot_nt(a, b):
    return lax.dot_general(a, b, (((1,), (1,)), ((), ())), preferred_element_type=F32)


def head_rows(values, group):
    width = values.shape[1]
    heads = range(group * GROUP_HEADS, (group + 1) * GROUP_HEADS)
    return jnp.concatenate(
        [jnp.broadcast_to(values[h : h + 1, :], (HEAD_DIM, width)) for h in heads], axis=0
    )


def head_column(values, group, width):
    heads = range(group * GROUP_HEADS, (group + 1) * GROUP_HEADS)
    return jnp.concatenate(
        [jnp.broadcast_to(values[h : h + 1, 0:1], (HEAD_DIM, width)) for h in heads], axis=0
    )


def write_spans(ref, first, span):
    high = span.astype(BF16).astype(F32)
    middle = (span - high).astype(BF16).astype(F32)
    low = span - high - middle
    lane = lax.broadcasted_iota(jnp.int32, span.shape, 1)
    parts = jnp.where(lane < 32, high, jnp.where(lane < 64, middle, low))
    ref[first : first + SPAN_ROWS, :] = parts.astype(BF16)


def read_spans(ref, first):
    parts = ref[first : first + SPAN_ROWS, :].astype(F32)
    span = parts[:, 0:1] + parts[:, 32:33] + parts[:, 64:65]
    return jnp.broadcast_to(span, (HEADS, STATE))


def state_kernel(listed, x_any, b_any, c_any, decay_any, weight_any, *rest):
    total_ref, pay_ref, start_ref, log_ref, far_ref, span_ref, x_ref, b_ref, c_ref, weight_ref = rest[:10]
    x_in, decay_ref, state, sems, x_sems = rest[10:]
    base = lax.axis_index("seq") * TOK_DEV
    resets = [listed[r] for r in range(RESETS)]
    decay_copy = pltpu.make_async_copy(decay_any, decay_ref, sems.at[0])
    b_copy = pltpu.make_async_copy(b_any, b_ref, sems.at[1])
    later = [
        pltpu.make_async_copy(c_any, c_ref, sems.at[2]),
        pltpu.make_async_copy(weight_any, weight_ref, sems.at[3]),
    ]
    x_copies = []
    for k in range(CHUNKS):
        rows = slice(k * CHUNK, (k + 1) * CHUNK)
        x_copies.append(pltpu.make_async_copy(x_any.at[rows, :], x_in.at[k], x_sems.at[k]))
    for copy in [decay_copy, b_copy] + x_copies[:AHEAD]:
        copy.start()
    state[...] = jnp.zeros_like(state)
    square = (CHUNK, CHUNK)
    upto = lax.broadcasted_iota(jnp.int32, square, 0) <= lax.broadcasted_iota(
        jnp.int32, square, 1
    )
    ones = upto.astype(F32).astype(BF16)
    decay_copy.wait()
    rows = jnp.concatenate(
        [decay_ref[:, k * CHUNK : (k + 1) * CHUNK] for k in range(CHUNKS)], axis=0
    )
    high = rows.astype(BF16)
    rest_of = rows - high.astype(F32)
    middle = rest_of.astype(BF16)
    low = (rest_of - middle.astype(F32)).astype(BF16)
    sums = dot(high, ones) + dot(middle, ones) + dot(low, ones)
    before = jnp.zeros((HEADS, 1), F32)
    b_copy.wait()
    for k in range(CHUNKS):
        log = sums[k * HEADS : (k + 1) * HEADS]
        lanes = slice(k * CHUNK, (k + 1) * CHUNK)
        end = log[:, CHUNK - 1 : CHUNK]
        first = base + k * CHUNK
        last = first + CHUNK - 1
        position = first + lax.broadcasted_iota(jnp.int32, (HEADS, CHUNK), 1)
        weight = jnp.exp(end - log)
        kept = jnp.exp(end)
        far = jnp.exp(before + log)
        for reset in resets:
            weight = jnp.where((position < reset) & (reset <= last), 0.0, weight)
            kept = jnp.where((reset >= first) & (reset <= last), 0.0, kept)
            far = jnp.where((reset >= base) & (position >= reset), 0.0, far)
        log_ref[:, lanes] = log
        far_ref[:, lanes] = far
        before = before + end
        if k == CHUNKS - 1:
            span_ref[...] = jnp.broadcast_to(far[:, CHUNK - 1 : CHUNK], (HEADS, STATE))
        middle = jnp.exp(0.5 * end)
        b = b_ref[lanes, :]
        x_copies[k].wait()
        if k + AHEAD < CHUNKS:
            x_copies[k + AHEAD].start()
        if k + AHEAD == CHUNKS - 1:
            for copy in later:
                copy.start()
        for group in range(GROUPS):
            rows = slice(group * WIDE, (group + 1) * WIDE)
            held = state[rows, :]
            start_ref[k, rows, :] = (held * head_column(middle, group, STATE)).astype(BF16)
            x = x_in[k, :, rows].T
            x_ref[k, rows, :] = x
            scaled = (x.astype(F32) * head_rows(weight, group)).astype(BF16)
            state[rows, :] = held * head_column(kept, group, STATE) + dot(scaled, b)
    total = state[...]
    total_ref[...] = total
    pay_ref[:FEATURES, :] = total.astype(BF16)
    write_spans(pay_ref, FEATURES, span_ref[...])
    for copy in later:
        copy.wait()


def block_states(resets, inputs, state_in, state_out, log_decay, level_weight):
    return pl.pallas_call(
        state_kernel,
        in_specs=[SMEM] + [ANY] * 5,
        out_specs=[VMEM] * 10,
        out_shape=[
            jax.ShapeDtypeStruct((FEATURES, STATE), F32),
            jax.ShapeDtypeStruct((FEATURES + SPAN_ROWS, STATE), BF16),
            jax.ShapeDtypeStruct((CHUNKS, FEATURES, STATE), BF16),
            jax.ShapeDtypeStruct((HEADS, TOK_DEV), F32),
            jax.ShapeDtypeStruct((HEADS, TOK_DEV), F32),
            jax.ShapeDtypeStruct((HEADS, STATE), F32),
            jax.ShapeDtypeStruct((CHUNKS, FEATURES, CHUNK), BF16),
            jax.ShapeDtypeStruct((TOK_DEV, STATE), BF16),
            jax.ShapeDtypeStruct((TOK_DEV, STATE), BF16),
            jax.ShapeDtypeStruct((LEVELS, HEADS, TOK_DEV), F32),
        ],
        scratch_shapes=[
            pltpu.VMEM((CHUNKS, CHUNK, FEATURES), BF16),
            pltpu.VMEM((HEADS, TOK_DEV), F32),
            pltpu.VMEM((FEATURES, STATE), F32),
            pltpu.SemaphoreType.DMA((4,)),
            pltpu.SemaphoreType.DMA((CHUNKS,)),
        ],
        compiler_params=pltpu.CompilerParams(**PARAMS),
        name="block_states",
    )(
        in_hbm(resets),
        in_hbm(inputs),
        in_hbm(state_in),
        in_hbm(state_out),
        in_hbm(log_decay),
        in_hbm(level_weight),
    )


def own_heads(span):
    return jnp.where(side(0) == 0, span[:HALF_HEADS], span[HALF_HEADS:])


def chip():
    return side(1)


def shard_head(span, head):
    row = side(0) * HALF_HEADS + chip() * SHARD_HEADS + head
    here = lax.broadcasted_iota(jnp.int32, span.shape, 0) == row
    return jnp.sum(jnp.where(here, span, 0.0), axis=0, keepdims=True)


def join_cores_kernel(own_ref, span_ref, got_ref, sum_ref, new_span_ref, new_lead_ref, factor_ref, pay_ref):
    upper = side(0) == 1
    span = span_ref[...]
    got_span = read_spans(got_ref, FEATURES)
    factor_ref[...] = jnp.broadcast_to(jnp.where(upper, 1.0, 0.0), span.shape)
    new_lead_ref[...] = jnp.where(upper, got_span, 1.0)
    both = span * got_span
    new_span_ref[...] = both
    own_factor = jnp.where(upper, 1.0, own_heads(got_span))
    got_factor = jnp.where(upper, own_heads(span), 1.0)
    for h in range(HALF_HEADS):
        rows = pl.ds(pl.multiple_of(side(0) * HALF + h * HEAD_DIM, HEAD_DIM), HEAD_DIM)
        got = got_ref[rows, :].astype(F32)
        new = own_ref[rows, :] * own_factor[h : h + 1] + got * got_factor[h : h + 1]
        here = slice(h * HEAD_DIM, (h + 1) * HEAD_DIM)
        sum_ref[here, :] = new
        pay_ref[here, :] = new.astype(BF16)
    write_spans(pay_ref, HALF, both)


def join_kernel(bit, own_ref, span_ref, lead_ref, got_ref, *rest):
    last = bit == 4
    if last:
        below, both_ref = rest[0], rest[1]
        both_ref[:SHARD, :] = below[:SHARD, :]
        both_ref[SHARD:, :] = got_ref[:SHARD, :]
    new_lead_ref, factor_ref, pay_ref = rest[-3:]
    upper = side(bit) == 1
    span, lead = span_ref[...], lead_ref[...]
    got_span = read_spans(got_ref, SHARD)
    factor_ref[...] = jnp.where(upper, lead, 0.0)
    new_lead_ref[...] = jnp.where(upper, lead * got_span, lead)
    both = span * got_span
    if not last:
        rest[1][...] = both
    for h in range(SHARD_HEADS):
        here = slice(h * HEAD_DIM, (h + 1) * HEAD_DIM)
        own_factor = jnp.where(upper, 1.0, shard_head(got_span, h))
        got_factor = jnp.where(upper, shard_head(span, h), 1.0)
        new = own_ref[here, :] * own_factor + got_ref[here, :].astype(F32) * got_factor
        if not last:
            rest[0][here, :] = new
        pay_ref[here, :] = new.astype(BF16)
    write_spans(pay_ref, SHARD, both)


SMALL = jax.ShapeDtypeStruct((HEADS, STATE), F32)
HALF_SUM = jax.ShapeDtypeStruct((HALF, STATE), F32)
HALF_PAY = jax.ShapeDtypeStruct((HALF + SPAN_ROWS, STATE), BF16)
SHARD_SUM = jax.ShapeDtypeStruct((SHARD, STATE), F32)
SHARD_PAIR = jax.ShapeDtypeStruct((2 * SHARD, STATE), BF16)
SHARD_PAY = jax.ShapeDtypeStruct((SHARD + SPAN_ROWS, STATE), BF16)


def join_cores(*operands):
    return pl.pallas_call(
        join_cores_kernel,
        in_specs=[VMEM] * len(operands),
        out_specs=[VMEM] * 5,
        out_shape=[HALF_SUM, SMALL, SMALL, SMALL, HALF_PAY],
        compiler_params=pltpu.CompilerParams(**PARAMS),
        name="join_cores",
    )(*operands)


def join(bit, *operands):
    return pl.pallas_call(
        functools.partial(join_kernel, bit),
        in_specs=[VMEM] * len(operands),
        out_specs=[VMEM] * (4 if bit == 4 else 5),
        out_shape=([SHARD_PAIR] if bit == 4 else [SHARD_SUM, SMALL]) + [SMALL, SMALL, SHARD_PAY],
        compiler_params=pltpu.CompilerParams(**PARAMS),
        name="join" + str(bit),
    )(*operands)


def gather_kernel(parts, *refs):
    out_ref = refs[-1]
    for distance in range(CHIPS):
        row = (chip() ^ distance) * SHARD
        for n in range(parts):
            rows = pl.ds(pl.multiple_of(row + n * HALF, SHARD), SHARD)
            out_ref[rows, :] = refs[distance][n * SHARD : (n + 1) * SHARD, :]


def gather(parts, own, got):
    return pl.pallas_call(
        functools.partial(gather_kernel, parts),
        in_specs=[VMEM] * CHIPS,
        out_specs=VMEM,
        out_shape=jax.ShapeDtypeStruct((parts * HALF, STATE), BF16),
        compiler_params=pltpu.CompilerParams(**PARAMS),
        name="gather" + str(parts),
    )(own, *got)


def join_chips_kernel(own_ref, span_ref, lead_ref, one_ref, two_ref, three_ref, *rest):
    sum_ref, new_span_ref, new_lead_ref, low_ref, high_ref, pay_ref, states_ref, sums = rest
    low_upper = side(1) == 1
    high_upper = side(2) == 1
    span, lead = span_ref[...], lead_ref[...]
    one, two, three = (read_spans(ref, HALF) for ref in (one_ref, two_ref, three_ref))
    low_ref[...] = jnp.where(low_upper, lead, 0.0)
    lead = jnp.where(low_upper, lead * one, lead)
    high_ref[...] = jnp.where(high_upper, lead, 0.0)
    near, away = span * one, two * three
    new_lead_ref[...] = jnp.where(high_upper, lead * away, lead)
    both = near * away
    new_span_ref[...] = both
    own_here = jnp.where(low_upper, 1.0, own_heads(one))
    one_here = jnp.where(low_upper, own_heads(span), 1.0)
    two_here = jnp.where(low_upper, 1.0, own_heads(three))
    three_here = jnp.where(low_upper, own_heads(two), 1.0)
    near_here = jnp.where(high_upper, 1.0, own_heads(away))
    away_here = jnp.where(high_upper, own_heads(near), 1.0)
    for h in range(HALF_HEADS):
        here = slice(h * HEAD_DIM, (h + 1) * HEAD_DIM)
        row = slice(h, h + 1)
        got = one_ref[here, :]
        here_sum = own_ref[here, :] * own_here[row] + got.astype(F32) * one_here[row]
        away_sum = two_ref[here, :].astype(F32) * two_here[row] + three_ref[here, :].astype(
            F32
        ) * three_here[row]
        new = here_sum * near_here[row] + away_sum * away_here[row]
        sums[here, :] = new
        states_ref[here, :] = got
        states_ref[HALF + h * HEAD_DIM : HALF + (h + 1) * HEAD_DIM, :] = away_sum.astype(BF16)
    shard = sums[pl.ds(pl.multiple_of(chip() * SHARD, SHARD), SHARD), :]
    sum_ref[...] = shard
    pay_ref[:SHARD, :] = shard.astype(BF16)
    write_spans(pay_ref, SHARD, both)


def join_chips(own, span, lead, got):
    return pl.pallas_call(
        join_chips_kernel,
        in_specs=[VMEM] * 6,
        out_specs=[VMEM] * 7,
        out_shape=[
            SHARD_SUM,
            SMALL,
            SMALL,
            SMALL,
            SMALL,
            SHARD_PAY,
            jax.ShapeDtypeStruct((FEATURES, STATE), BF16),
        ],
        scratch_shapes=[pltpu.VMEM((HALF, STATE), F32)],
        compiler_params=pltpu.CompilerParams(**PARAMS),
        name="join_chips",
    )(own, span, lead, *got)


LATER = LEVELS - 2


def inner_kernel(chunks, listed, skip, x_ref, b_ref, c_ref, log_ref, weight_ref, far_ref, start_ref, got_ref, factor_ref, *rest):
    y_ref, flipped_ref, coef_ref = rest[-3:]
    square = (CHUNK, CHUNK)
    for chunk in chunks:
        first = lax.axis_index("seq") * TOK_DEV + chunk * CHUNK
        lanes = slice(chunk * CHUNK, (chunk + 1) * CHUNK)
        log = log_ref[:, lanes]
        far = far_ref[:, lanes]
        middle = 0.5 * log[:, CHUNK - 1 : CHUNK]
        after = weight_ref[0, :, lanes] * jnp.exp(log - middle)
        before = jnp.exp(middle - log)
        level = weight_ref[1, :, lanes] * far * factor_ref[:, 0:1]
        for n in range(LATER):
            coef_ref[n, :, lanes] = weight_ref[2 + n, :, lanes] * far
        source = first + lax.broadcasted_iota(jnp.int32, square, 0)
        target = first + lax.broadcasted_iota(jnp.int32, square, 1)
        c = c_ref[lanes, :].T
        flipped_ref[:, lanes] = c
        scores = dot(b_ref[lanes, :], c)
        scores = jnp.where(source <= target, scores, 0.0)
        reached = first + lax.broadcasted_iota(jnp.int32, (STATE, CHUNK), 1)
        near = c.astype(F32)
        for r in range(RESETS):
            reset = listed[r]
            scores = jnp.where((source < reset) & (reset <= target), 0.0, scores)
            near = jnp.where((reset >= first) & (reached >= reset), 0.0, near)
        scores = scores.astype(BF16)
        near = near.astype(BF16)
        for group in range(GROUPS):
            rows = slice(group * WIDE, (group + 1) * WIDE)
            x = x_ref[chunk, rows, :].astype(F32)
            scaled = (x * head_rows(before, group)).astype(BF16)
            inside = dot(scaled, scores) + dot(start_ref[chunk, rows, :], near)
            y = inside * head_rows(after, group)
            y = y + dot(got_ref[rows, :], c) * head_rows(level, group)
            direct = jnp.concatenate(
                [
                    x[h * HEAD_DIM : (h + 1) * HEAD_DIM] * skip[group * GROUP_HEADS + h]
                    for h in range(GROUP_HEADS)
                ],
                axis=0,
            )
            y_ref[chunk, rows, :] = y + direct


def inner(chunk0, operands, parts):
    resets, skip, *others = operands
    operands = [in_hbm(resets), in_hbm(skip)] + others
    in_specs = [SMEM, SMEM] + [VMEM] * len(others)
    aliases = {}
    if parts is not None:
        aliases = {len(operands) + n: n for n in range(3)}
        operands += parts
        in_specs += [VMEM] * 3
    return list(
        pl.pallas_call(
            functools.partial(inner_kernel, range(chunk0, chunk0 + PIECE)),
            in_specs=in_specs,
            out_specs=[VMEM] * 3,
            out_shape=[
                jax.ShapeDtypeStruct((CHUNKS, FEATURES, CHUNK), F32),
                jax.ShapeDtypeStruct((STATE, TOK_DEV), BF16),
                jax.ShapeDtypeStruct((LATER, HEADS, TOK_DEV), F32),
            ],
            input_output_aliases=aliases,
            compiler_params=pltpu.CompilerParams(**PARAMS),
            cost_estimate=pl.CostEstimate(
                flops=PIECE * 2 * CHUNK * FEATURES * 768, bytes_accessed=PIECE * 2_000_000, transcendentals=0
            ),
            name="inner" + str(chunk0),
        )(*operands)
    )


def level_kernel(levels, parts, final, flipped_ref, coef_ref, *rest):
    count = len(levels)
    mine, other = rest[:parts], rest[parts : 2 * parts]
    factors = rest[2 * parts : 2 * parts + count]
    y_ref, states = rest[-2 - final], rest[-1]
    lower = side(0) == 0
    factors = [factor[:, 0:1] for factor in factors]
    if final:
        factors = [jnp.where(side(LEVELS - 2) == 1, factor, 0.0) for factor in factors]
    for n in range(count):
        part, start = (0, n * HALF) if parts == 1 else (n, 0)
        a = mine[part][start : start + HALF, :].astype(F32)
        b = other[part][start : start + HALF, :].astype(F32)
        states[n, :HALF, :] = jnp.where(lower, a, b).astype(BF16)
        states[n, HALF:, :] = jnp.where(lower, b, a).astype(BF16)
    for chunk in range(CHUNKS):
        lanes = slice(chunk * CHUNK, (chunk + 1) * CHUNK)
        coefs = [coef_ref[level - 2, :, lanes] * factors[n] for n, level in enumerate(levels)]
        c = flipped_ref[:, lanes]
        squares = jnp.zeros((8, CHUNK), F32)
        for group in range(GROUPS):
            rows = slice(group * WIDE, (group + 1) * WIDE)
            y = y_ref[chunk, rows, :]
            for n in range(count):
                y = y + dot(states[n, rows, :], c) * head_rows(coefs[n], group)
            y_ref[chunk, rows, :] = y
            if final:
                part = y * y
                for k in range(WIDE // 8):
                    squares = squares + part[8 * k : 8 * k + 8]
        if final:
            rest[-2][chunk] = jnp.sum(squares, axis=0, keepdims=True)


def add_levels(levels, final, mine, other, factors, y, flipped, coef):
    count = len(levels)
    operands = [flipped, coef, *mine, *other, *factors]
    return pl.pallas_call(
        functools.partial(level_kernel, levels, len(mine), final),
        in_specs=[VMEM] * (len(operands) + 1),
        out_specs=[VMEM] * (1 + final),
        out_shape=[
            jax.ShapeDtypeStruct((CHUNKS, FEATURES, CHUNK), F32),
            jax.ShapeDtypeStruct((CHUNKS, 1, CHUNK), F32),
        ][: 1 + final],
        input_output_aliases={len(operands): 0},
        scratch_shapes=[pltpu.VMEM((count, FEATURES, STATE), BF16)],
        compiler_params=pltpu.CompilerParams(**PARAMS),
        cost_estimate=pl.CostEstimate(
            flops=count * 4 * TOK_DEV * FEATURES * STATE, bytes_accessed=4_000_000, transcendentals=0
        ),
        name="levels" + str(levels[0]),
    )(*operands, y)


def flip_kernel(y_ref, gain_ref, out_ref):
    for chunk in range(CHUNKS):
        for group in range(GROUPS):
            rows = slice(group * WIDE, (group + 1) * WIDE)
            y = y_ref[chunk, rows, :].T
            out_ref[chunk * CHUNK : (chunk + 1) * CHUNK, rows] = y * gain_ref[:, rows]


def flip(y, gain):
    return pl.pallas_call(
        flip_kernel,
        in_specs=[VMEM] * 2,
        out_specs=VMEM,
        out_shape=jax.ShapeDtypeStruct((TOK_DEV, FEATURES), F32),
        compiler_params=pltpu.CompilerParams(**PARAMS),
        cost_estimate=pl.CostEstimate(flops=0, bytes_accessed=16_000_000, transcendentals=0),
        name="flip",
    )(y, gain)


def norm_kernel(y_ref, s0, s1, s2, s3, out_any, buffers, sems):
    copies = []
    for chunk in range(CHUNKS):
        rows = slice(chunk * CHUNK, (chunk + 1) * CHUNK)
        squares = (s0[chunk] + s1[chunk]) + (s2[chunk] + s3[chunk])
        scale = lax.rsqrt(squares * (1.0 / (HEAD_TOTAL * HEAD_DIM)) + EPSILON)
        scale = jnp.broadcast_to(scale, (STATE, CHUNK)).T
        for column in range(FEATURES // STATE):
            columns = slice(column * STATE, (column + 1) * STATE)
            buffers[rows, columns] = (y_ref[rows, columns] * scale).astype(BF16)
        copies.append(
            pltpu.make_async_copy(buffers.at[rows, :], out_any.at[rows, :], sems.at[chunk])
        )
        copies[chunk].start()
    for copy in copies:
        copy.wait()


def normalize(y, squares):
    return pl.pallas_call(
        norm_kernel,
        in_specs=[VMEM] * 5,
        out_specs=ANY,
        out_shape=jax.ShapeDtypeStruct((TOK_DEV, FEATURES), BF16),
        scratch_shapes=[
            pltpu.VMEM((TOK_DEV, FEATURES), BF16),
            pltpu.SemaphoreType.DMA((CHUNKS,)),
        ],
        compiler_params=pltpu.CompilerParams(**PARAMS),
        name="normalize",
    )(y, *squares)


def swap(array, axis, distance, only_up=None):
    count = lax.axis_size(axis)
    route = [
        (low, low ^ distance)
        for low in range(count)
        if only_up is None or not low >> only_up & 1
    ]
    return lax.ppermute(array, axis, route)


def per_device(inputs, state_in, state_out, log_decay, level_weight, skip, norm_gain, resets):
    total, pay, starts, log, far, span, x, b, c, weights = block_states(
        resets, inputs, state_in, state_out, log_decay, level_weight
    )
    one = swap(pay, "seq", 1)
    half, span, lead, one_factor, pay = join_cores(total, span, one)
    within = (resets, skip, x, b, c, log, weights, far, starts, one, one_factor)
    got = [swap(pay, "seq", distance) for distance in (2, 6, 4)]
    parts = inner(0, within, None)
    parts = inner(2, within, parts)
    got, parts = lax.optimization_barrier((got, parts))
    shard, span, lead, two_factor, three_factor, pay, mine = join_chips(
        half, span, lead, (got[0], got[2], got[1])
    )
    four = swap(pay, "seq", 8)
    mine, pay = lax.optimization_barrier((mine, pay))
    other = swap(mine, "seq", 1)
    parts = inner(4, within, parts)
    four, parts = lax.optimization_barrier((four, parts))
    shard, span, lead, four_factor, pay = join(3, shard, span, lead, four)
    five = swap(pay, "seq", 16)
    pay, parts = lax.optimization_barrier((pay, parts))
    parts = inner(6, within, parts)
    y, flipped, coef = parts
    (y,) = add_levels((2, 3), False, [mine], [other], [two_factor, three_factor], y, flipped, coef)
    five, y = lax.optimization_barrier((five, y))
    both, lead, five_factor, pay = join(4, shard, span, lead, five, four)
    six = swap(pay, "seq", 48)
    both, y = lax.optimization_barrier((both, y))
    both_got = swap(both, "seq", 2)
    both_got, six, y = lax.optimization_barrier((both_got, six, y))
    six_got = swap(six, "seq", 2)
    mine = gather(2, both, [both_got])
    other = swap(mine, "seq", 1)
    (y,) = add_levels((4, 5), False, [mine], [other], [four_factor, five_factor], y, flipped, coef)
    six_got, y = lax.optimization_barrier((six_got, y))
    mine = gather(1, six, [six_got])
    other = swap(mine, "seq", 1)
    y, squares = add_levels((6,), True, [mine], [other], [lead], y, flipped, coef)
    shares = [squares] + [
        lax.ppermute(squares, "head", [(i, i ^ d) for i in range(4)]) for d in (1, 3, 2)
    ]
    return normalize(flip(y, norm_gain.reshape(1, FEATURES)), shares)


def solution(mesh):
    placed = (
        P("seq", "head"),
        P("seq", None),
        P("seq", None),
        P("head", "seq"),
        P(None, "head", "seq"),
        P("head"),
        P("head"),
        P(),
    )
    return jax.shard_map(
        per_device, mesh=mesh, in_specs=placed, out_specs=P("seq", "head"), check_vma=False
    )
```

```python
import functools

import jax
import jax.numpy as jnp
from jax import lax
from jax.experimental import pallas as pl
from jax.experimental.pallas import tpu as pltpu
from jax.sharding import PartitionSpec as P

HEAD_TOTAL = 64
HEAD_DIM = 64
STATE = 128
LEVELS = 7
TOK_DEV = 2048
EPSILON = 1e-05

CHUNK = 256
CHUNKS = TOK_DEV // CHUNK
HEADS = 16
FEATURES = HEADS * HEAD_DIM
HALF = FEATURES // 2
HALF_HEADS = HEADS // 2
CHIPS = 2
SHARD = HALF // CHIPS
SHARD_HEADS = HALF_HEADS // CHIPS
GROUP_HEADS = 8
AHEAD = 3
WIDE = GROUP_HEADS * HEAD_DIM
GROUPS = HEADS // GROUP_HEADS
SPAN_ROWS = HEADS
RESETS = 4
PIECE = 2

F32 = jnp.float32
BF16 = jnp.bfloat16
PARAMS = dict(vmem_limit_bytes=16 * 1024 * 1024)
SMEM = pl.BlockSpec(memory_space=pltpu.SMEM)
VMEM = pl.BlockSpec(memory_space=pltpu.VMEM)
ANY = pl.BlockSpec(memory_space=pl.ANY)


def side(bit):
    return lax.axis_index("seq") >> bit & 1


def in_hbm(array):
    return pltpu.with_memory_space_constraint(array, pltpu.HBM)


def dot(a, b):
    return lax.dot_general(a, b, (((1,), (0,)), ((), ())), preferred_element_type=F32)


def dot_nt(a, b):
    return lax.dot_general(a, b, (((1,), (1,)), ((), ())), preferred_element_type=F32)


def head_rows(values, group):
    width = values.shape[1]
    heads = range(group * GROUP_HEADS, (group + 1) * GROUP_HEADS)
    return jnp.concatenate(
        [jnp.broadcast_to(values[h : h + 1, :], (HEAD_DIM, width)) for h in heads], axis=0
    )


def head_column(values, group, width):
    heads = range(group * GROUP_HEADS, (group + 1) * GROUP_HEADS)
    return jnp.concatenate(
        [jnp.broadcast_to(values[h : h + 1, 0:1], (HEAD_DIM, width)) for h in heads], axis=0
    )


def write_spans(ref, first, span):
    high = span.astype(BF16).astype(F32)
    middle = (span - high).astype(BF16).astype(F32)
    low = span - high - middle
    lane = lax.broadcasted_iota(jnp.int32, span.shape, 1)
    parts = jnp.where(lane < 32, high, jnp.where(lane < 64, middle, low))
    ref[first : first + SPAN_ROWS, :] = parts.astype(BF16)


def read_spans(ref, first):
    parts = ref[first : first + SPAN_ROWS, :].astype(F32)
    span = parts[:, 0:1] + parts[:, 32:33] + parts[:, 64:65]
    return jnp.broadcast_to(span, (HEADS, STATE))


def state_kernel(listed, x_any, b_any, c_any, decay_any, weight_any, *rest):
    total_ref, pay_ref, start_ref, log_ref, far_ref, span_ref, x_ref, b_ref, c_ref, weight_ref = rest[:10]
    x_in, decay_ref, state, sems, x_sems = rest[10:]
    base = lax.axis_index("seq") * TOK_DEV
    resets = [listed[r] for r in range(RESETS)]
    decay_copy = pltpu.make_async_copy(decay_any, decay_ref, sems.at[0])
    b_copy = pltpu.make_async_copy(b_any, b_ref, sems.at[1])
    later = [
        pltpu.make_async_copy(c_any, c_ref, sems.at[2]),
        pltpu.make_async_copy(weight_any, weight_ref, sems.at[3]),
    ]
    x_copies = []
    for k in range(CHUNKS):
        rows = slice(k * CHUNK, (k + 1) * CHUNK)
        x_copies.append(pltpu.make_async_copy(x_any.at[rows, :], x_in.at[k], x_sems.at[k]))
    for copy in [decay_copy, b_copy] + x_copies[:AHEAD]:
        copy.start()
    state[...] = jnp.zeros_like(state)
    square = (CHUNK, CHUNK)
    upto = lax.broadcasted_iota(jnp.int32, square, 0) <= lax.broadcasted_iota(
        jnp.int32, square, 1
    )
    ones = upto.astype(F32).astype(BF16)
    decay_copy.wait()
    rows = jnp.concatenate(
        [decay_ref[:, k * CHUNK : (k + 1) * CHUNK] for k in range(CHUNKS)], axis=0
    )
    high = rows.astype(BF16)
    rest_of = rows - high.astype(F32)
    middle = rest_of.astype(BF16)
    low = (rest_of - middle.astype(F32)).astype(BF16)
    sums = dot(high, ones) + dot(middle, ones) + dot(low, ones)
    before = jnp.zeros((HEADS, 1), F32)
    b_copy.wait()
    for k in range(CHUNKS):
        log = sums[k * HEADS : (k + 1) * HEADS]
        lanes = slice(k * CHUNK, (k + 1) * CHUNK)
        end = log[:, CHUNK - 1 : CHUNK]
        first = base + k * CHUNK
        last = first + CHUNK - 1
        position = first + lax.broadcasted_iota(jnp.int32, (HEADS, CHUNK), 1)
        weight = jnp.exp(end - log)
        kept = jnp.exp(end)
        far = jnp.exp(before + log)
        for reset in resets:
            weight = jnp.where((position < reset) & (reset <= last), 0.0, weight)
            kept = jnp.where((reset >= first) & (reset <= last), 0.0, kept)
            far = jnp.where((reset >= base) & (position >= reset), 0.0, far)
        log_ref[:, lanes] = log
        far_ref[:, lanes] = far
        before = before + end
        if k == CHUNKS - 1:
            span_ref[...] = jnp.broadcast_to(far[:, CHUNK - 1 : CHUNK], (HEADS, STATE))
        middle = jnp.exp(0.5 * end)
        b = b_ref[lanes, :]
        x_copies[k].wait()
        if k + AHEAD < CHUNKS:
            x_copies[k + AHEAD].start()
        if k + AHEAD == CHUNKS - 1:
            for copy in later:
                copy.start()
        for group in range(GROUPS):
            rows = slice(group * WIDE, (group + 1) * WIDE)
            held = state[rows, :]
            start_ref[k, rows, :] = (held * head_column(middle, group, STATE)).astype(BF16)
            x = x_in[k, :, rows].T
            x_ref[k, rows, :] = x
            scaled = (x.astype(F32) * head_rows(weight, group)).astype(BF16)
            state[rows, :] = held * head_column(kept, group, STATE) + dot(scaled, b)
    total = state[...]
    total_ref[...] = total
    pay_ref[:FEATURES, :] = total.astype(BF16)
    write_spans(pay_ref, FEATURES, span_ref[...])
    for copy in later:
        copy.wait()


def block_states(resets, inputs, state_in, state_out, log_decay, level_weight):
    return pl.pallas_call(
        state_kernel,
        in_specs=[SMEM] + [ANY] * 5,
        out_specs=[VMEM] * 10,
        out_shape=[
            jax.ShapeDtypeStruct((FEATURES, STATE), F32),
            jax.ShapeDtypeStruct((FEATURES + SPAN_ROWS, STATE), BF16),
            jax.ShapeDtypeStruct((CHUNKS, FEATURES, STATE), BF16),
            jax.ShapeDtypeStruct((HEADS, TOK_DEV), F32),
            jax.ShapeDtypeStruct((HEADS, TOK_DEV), F32),
            jax.ShapeDtypeStruct((HEADS, STATE), F32),
            jax.ShapeDtypeStruct((CHUNKS, FEATURES, CHUNK), BF16),
            jax.ShapeDtypeStruct((TOK_DEV, STATE), BF16),
            jax.ShapeDtypeStruct((TOK_DEV, STATE), BF16),
            jax.ShapeDtypeStruct((LEVELS, HEADS, TOK_DEV), F32),
        ],
        scratch_shapes=[
            pltpu.VMEM((CHUNKS, CHUNK, FEATURES), BF16),
            pltpu.VMEM((HEADS, TOK_DEV), F32),
            pltpu.VMEM((FEATURES, STATE), F32),
            pltpu.SemaphoreType.DMA((4,)),
            pltpu.SemaphoreType.DMA((CHUNKS,)),
        ],
        compiler_params=pltpu.CompilerParams(**PARAMS),
        name="block_states",
    )(
        in_hbm(resets),
        in_hbm(inputs),
        in_hbm(state_in),
        in_hbm(state_out),
        in_hbm(log_decay),
        in_hbm(level_weight),
    )


def own_heads(span):
    return jnp.where(side(0) == 0, span[:HALF_HEADS], span[HALF_HEADS:])


def chip():
    return side(1)


def shard_head(span, head):
    row = side(0) * HALF_HEADS + chip() * SHARD_HEADS + head
    here = lax.broadcasted_iota(jnp.int32, span.shape, 0) == row
    return jnp.sum(jnp.where(here, span, 0.0), axis=0, keepdims=True)


def join_cores_kernel(own_ref, span_ref, got_ref, sum_ref, new_span_ref, new_lead_ref, factor_ref, pay_ref):
    upper = side(0) == 1
    span = span_ref[...]
    got_span = read_spans(got_ref, FEATURES)
    factor_ref[...] = jnp.broadcast_to(jnp.where(upper, 1.0, 0.0), span.shape)
    new_lead_ref[...] = jnp.where(upper, got_span, 1.0)
    both = span * got_span
    new_span_ref[...] = both
    own_factor = jnp.where(upper, 1.0, own_heads(got_span))
    got_factor = jnp.where(upper, own_heads(span), 1.0)
    for h in range(HALF_HEADS):
        rows = pl.ds(pl.multiple_of(side(0) * HALF + h * HEAD_DIM, HEAD_DIM), HEAD_DIM)
        got = got_ref[rows, :].astype(F32)
        new = own_ref[rows, :] * own_factor[h : h + 1] + got * got_factor[h : h + 1]
        here = slice(h * HEAD_DIM, (h + 1) * HEAD_DIM)
        sum_ref[here, :] = new
        pay_ref[here, :] = new.astype(BF16)
    write_spans(pay_ref, HALF, both)


def join_kernel(bit, own_ref, span_ref, lead_ref, got_ref, *rest):
    last = bit == 4
    if last:
        below, both_ref = rest[0], rest[1]
        both_ref[:SHARD, :] = below[:SHARD, :]
        both_ref[SHARD:, :] = got_ref[:SHARD, :]
    new_lead_ref, factor_ref, pay_ref = rest[-3:]
    upper = side(bit) == 1
    span, lead = span_ref[...], lead_ref[...]
    got_span = read_spans(got_ref, SHARD)
    factor_ref[...] = jnp.where(upper, lead, 0.0)
    new_lead_ref[...] = jnp.where(upper, lead * got_span, lead)
    both = span * got_span
    if not last:
        rest[1][...] = both
    for h in range(SHARD_HEADS):
        here = slice(h * HEAD_DIM, (h + 1) * HEAD_DIM)
        own_factor = jnp.where(upper, 1.0, shard_head(got_span, h))
        got_factor = jnp.where(upper, shard_head(span, h), 1.0)
        new = own_ref[here, :] * own_factor + got_ref[here, :].astype(F32) * got_factor
        if not last:
            rest[0][here, :] = new
        pay_ref[here, :] = new.astype(BF16)
    write_spans(pay_ref, SHARD, both)


SMALL = jax.ShapeDtypeStruct((HEADS, STATE), F32)
HALF_SUM = jax.ShapeDtypeStruct((HALF, STATE), F32)
HALF_PAY = jax.ShapeDtypeStruct((HALF + SPAN_ROWS, STATE), BF16)
SHARD_SUM = jax.ShapeDtypeStruct((SHARD, STATE), F32)
SHARD_PAIR = jax.ShapeDtypeStruct((2 * SHARD, STATE), BF16)
SHARD_PAY = jax.ShapeDtypeStruct((SHARD + SPAN_ROWS, STATE), BF16)


def join_cores(*operands):
    return pl.pallas_call(
        join_cores_kernel,
        in_specs=[VMEM] * len(operands),
        out_specs=[VMEM] * 5,
        out_shape=[HALF_SUM, SMALL, SMALL, SMALL, HALF_PAY],
        compiler_params=pltpu.CompilerParams(**PARAMS),
        name="join_cores",
    )(*operands)


def join(bit, *operands):
    return pl.pallas_call(
        functools.partial(join_kernel, bit),
        in_specs=[VMEM] * len(operands),
        out_specs=[VMEM] * (4 if bit == 4 else 5),
        out_shape=([SHARD_PAIR] if bit == 4 else [SHARD_SUM, SMALL]) + [SMALL, SMALL, SHARD_PAY],
        compiler_params=pltpu.CompilerParams(**PARAMS),
        name="join" + str(bit),
    )(*operands)


def gather_kernel(parts, *refs):
    out_ref = refs[-1]
    for distance in range(CHIPS):
        row = (chip() ^ distance) * SHARD
        for n in range(parts):
            rows = pl.ds(pl.multiple_of(row + n * HALF, SHARD), SHARD)
            out_ref[rows, :] = refs[distance][n * SHARD : (n + 1) * SHARD, :]


def gather(parts, own, got):
    return pl.pallas_call(
        functools.partial(gather_kernel, parts),
        in_specs=[VMEM] * CHIPS,
        out_specs=VMEM,
        out_shape=jax.ShapeDtypeStruct((parts * HALF, STATE), BF16),
        compiler_params=pltpu.CompilerParams(**PARAMS),
        name="gather" + str(parts),
    )(own, *got)


def join_chips_kernel(own_ref, span_ref, lead_ref, one_ref, two_ref, three_ref, *rest):
    sum_ref, new_span_ref, new_lead_ref, low_ref, high_ref, pay_ref, states_ref, sums = rest
    low_upper = side(1) == 1
    high_upper = side(2) == 1
    span, lead = span_ref[...], lead_ref[...]
    one, two, three = (read_spans(ref, HALF) for ref in (one_ref, two_ref, three_ref))
    low_ref[...] = jnp.where(low_upper, lead, 0.0)
    lead = jnp.where(low_upper, lead * one, lead)
    high_ref[...] = jnp.where(high_upper, lead, 0.0)
    near, away = span * one, two * three
    new_lead_ref[...] = jnp.where(high_upper, lead * away, lead)
    both = near * away
    new_span_ref[...] = both
    own_here = jnp.where(low_upper, 1.0, own_heads(one))
    one_here = jnp.where(low_upper, own_heads(span), 1.0)
    two_here = jnp.where(low_upper, 1.0, own_heads(three))
    three_here = jnp.where(low_upper, own_heads(two), 1.0)
    near_here = jnp.where(high_upper, 1.0, own_heads(away))
    away_here = jnp.where(high_upper, own_heads(near), 1.0)
    for h in range(HALF_HEADS):
        here = slice(h * HEAD_DIM, (h + 1) * HEAD_DIM)
        row = slice(h, h + 1)
        got = one_ref[here, :]
        here_sum = own_ref[here, :] * own_here[row] + got.astype(F32) * one_here[row]
        away_sum = two_ref[here, :].astype(F32) * two_here[row] + three_ref[here, :].astype(
            F32
        ) * three_here[row]
        new = here_sum * near_here[row] + away_sum * away_here[row]
        sums[here, :] = new
        states_ref[here, :] = got
        states_ref[HALF + h * HEAD_DIM : HALF + (h + 1) * HEAD_DIM, :] = away_sum.astype(BF16)
    shard = sums[pl.ds(pl.multiple_of(chip() * SHARD, SHARD), SHARD), :]
    sum_ref[...] = shard
    pay_ref[:SHARD, :] = shard.astype(BF16)
    write_spans(pay_ref, SHARD, both)


def join_chips(own, span, lead, got):
    return pl.pallas_call(
        join_chips_kernel,
        in_specs=[VMEM] * 6,
        out_specs=[VMEM] * 7,
        out_shape=[
            SHARD_SUM,
            SMALL,
            SMALL,
            SMALL,
            SMALL,
            SHARD_PAY,
            jax.ShapeDtypeStruct((FEATURES, STATE), BF16),
        ],
        scratch_shapes=[pltpu.VMEM((HALF, STATE), F32)],
        compiler_params=pltpu.CompilerParams(**PARAMS),
        name="join_chips",
    )(own, span, lead, *got)


LATER = LEVELS - 2


def inner_kernel(chunks, listed, skip, x_ref, b_ref, c_ref, log_ref, weight_ref, far_ref, start_ref, got_ref, factor_ref, *rest):
    y_ref, flipped_ref, coef_ref = rest[-3:]
    square = (CHUNK, CHUNK)
    for chunk in chunks:
        first = lax.axis_index("seq") * TOK_DEV + chunk * CHUNK
        lanes = slice(chunk * CHUNK, (chunk + 1) * CHUNK)
        log = log_ref[:, lanes]
        far = far_ref[:, lanes]
        middle = 0.5 * log[:, CHUNK - 1 : CHUNK]
        after = weight_ref[0, :, lanes] * jnp.exp(log - middle)
        before = jnp.exp(middle - log)
        level = weight_ref[1, :, lanes] * far * factor_ref[:, 0:1]
        for n in range(LATER):
            coef_ref[n, :, lanes] = weight_ref[2 + n, :, lanes] * far
        source = first + lax.broadcasted_iota(jnp.int32, square, 0)
        target = first + lax.broadcasted_iota(jnp.int32, square, 1)
        c = c_ref[lanes, :].T
        flipped_ref[:, lanes] = c
        scores = dot(b_ref[lanes, :], c)
        scores = jnp.where(source <= target, scores, 0.0)
        reached = first + lax.broadcasted_iota(jnp.int32, (STATE, CHUNK), 1)
        near = c.astype(F32)
        for r in range(RESETS):
            reset = listed[r]
            scores = jnp.where((source < reset) & (reset <= target), 0.0, scores)
            near = jnp.where((reset >= first) & (reached >= reset), 0.0, near)
        scores = scores.astype(BF16)
        near = near.astype(BF16)
        for group in range(GROUPS):
            rows = slice(group * WIDE, (group + 1) * WIDE)
            x = x_ref[chunk, rows, :].astype(F32)
            scaled = (x * head_rows(before, group)).astype(BF16)
            inside = dot(scaled, scores) + dot(start_ref[chunk, rows, :], near)
            y = inside * head_rows(after, group)
            y = y + dot(got_ref[rows, :], c) * head_rows(level, group)
            direct = jnp.concatenate(
                [
                    x[h * HEAD_DIM : (h + 1) * HEAD_DIM] * skip[group * GROUP_HEADS + h]
                    for h in range(GROUP_HEADS)
                ],
                axis=0,
            )
            y_ref[chunk, rows, :] = y + direct


def inner(chunk0, operands, parts):
    resets, skip, *others = operands
    operands = [in_hbm(resets), in_hbm(skip)] + others
    in_specs = [SMEM, SMEM] + [VMEM] * len(others)
    aliases = {}
    if parts is not None:
        aliases = {len(operands) + n: n for n in range(3)}
        operands += parts
        in_specs += [VMEM] * 3
    return list(
        pl.pallas_call(
            functools.partial(inner_kernel, range(chunk0, chunk0 + PIECE)),
            in_specs=in_specs,
            out_specs=[VMEM] * 3,
            out_shape=[
                jax.ShapeDtypeStruct((CHUNKS, FEATURES, CHUNK), F32),
                jax.ShapeDtypeStruct((STATE, TOK_DEV), BF16),
                jax.ShapeDtypeStruct((LATER, HEADS, TOK_DEV), F32),
            ],
            input_output_aliases=aliases,
            compiler_params=pltpu.CompilerParams(**PARAMS),
            cost_estimate=pl.CostEstimate(
                flops=PIECE * 2 * CHUNK * FEATURES * 768, bytes_accessed=PIECE * 2_000_000, transcendentals=0
            ),
            name="inner" + str(chunk0),
        )(*operands)
    )


def level_kernel(levels, parts, final, flipped_ref, coef_ref, *rest):
    count = len(levels)
    mine, other = rest[:parts], rest[parts : 2 * parts]
    factors = rest[2 * parts : 2 * parts + count]
    y_ref, states = rest[-2 - final], rest[-1]
    lower = side(0) == 0
    factors = [factor[:, 0:1] for factor in factors]
    if final:
        factors = [jnp.where(side(LEVELS - 2) == 1, factor, 0.0) for factor in factors]
    for n in range(count):
        part, start = (0, n * HALF) if parts == 1 else (n, 0)
        a = mine[part][start : start + HALF, :].astype(F32)
        b = other[part][start : start + HALF, :].astype(F32)
        states[n, :HALF, :] = jnp.where(lower, a, b).astype(BF16)
        states[n, HALF:, :] = jnp.where(lower, b, a).astype(BF16)
    for chunk in range(CHUNKS):
        lanes = slice(chunk * CHUNK, (chunk + 1) * CHUNK)
        coefs = [coef_ref[level - 2, :, lanes] * factors[n] for n, level in enumerate(levels)]
        c = flipped_ref[:, lanes]
        squares = jnp.zeros((8, CHUNK), F32)
        for group in range(GROUPS):
            rows = slice(group * WIDE, (group + 1) * WIDE)
            y = y_ref[chunk, rows, :]
            for n in range(count):
                y = y + dot(states[n, rows, :], c) * head_rows(coefs[n], group)
            y_ref[chunk, rows, :] = y
            if final:
                part = y * y
                for k in range(WIDE // 8):
                    squares = squares + part[8 * k : 8 * k + 8]
        if final:
            rest[-2][chunk] = jnp.sum(squares, axis=0, keepdims=True)


def add_levels(levels, final, mine, other, factors, y, flipped, coef):
    count = len(levels)
    operands = [flipped, coef, *mine, *other, *factors]
    return pl.pallas_call(
        functools.partial(level_kernel, levels, len(mine), final),
        in_specs=[VMEM] * (len(operands) + 1),
        out_specs=[VMEM] * (1 + final),
        out_shape=[
            jax.ShapeDtypeStruct((CHUNKS, FEATURES, CHUNK), F32),
            jax.ShapeDtypeStruct((CHUNKS, 1, CHUNK), F32),
        ][: 1 + final],
        input_output_aliases={len(operands): 0},
        scratch_shapes=[pltpu.VMEM((count, FEATURES, STATE), BF16)],
        compiler_params=pltpu.CompilerParams(**PARAMS),
        cost_estimate=pl.CostEstimate(
            flops=count * 4 * TOK_DEV * FEATURES * STATE, bytes_accessed=4_000_000, transcendentals=0
        ),
        name="levels" + str(levels[0]),
    )(*operands, y)


def flip_kernel(y_ref, gain_ref, out_ref):
    for chunk in range(CHUNKS):
        for group in range(GROUPS):
            rows = slice(group * WIDE, (group + 1) * WIDE)
            y = y_ref[chunk, rows, :].T
            out_ref[chunk * CHUNK : (chunk + 1) * CHUNK, rows] = y * gain_ref[:, rows]


def flip(y, gain):
    return pl.pallas_call(
        flip_kernel,
        in_specs=[VMEM] * 2,
        out_specs=VMEM,
        out_shape=jax.ShapeDtypeStruct((TOK_DEV, FEATURES), F32),
        compiler_params=pltpu.CompilerParams(**PARAMS),
        cost_estimate=pl.CostEstimate(flops=0, bytes_accessed=16_000_000, transcendentals=0),
        name="flip",
    )(y, gain)


def norm_kernel(y_ref, s0, s1, s2, s3, out_any, buffers, sems):
    copies = []
    for chunk in range(CHUNKS):
        rows = slice(chunk * CHUNK, (chunk + 1) * CHUNK)
        squares = (s0[chunk] + s1[chunk]) + (s2[chunk] + s3[chunk])
        scale = lax.rsqrt(squares * (1.0 / (HEAD_TOTAL * HEAD_DIM)) + EPSILON)
        scale = jnp.broadcast_to(scale, (STATE, CHUNK)).T
        for column in range(FEATURES // STATE):
            columns = slice(column * STATE, (column + 1) * STATE)
            buffers[rows, columns] = (y_ref[rows, columns] * scale).astype(BF16)
        copies.append(
            pltpu.make_async_copy(buffers.at[rows, :], out_any.at[rows, :], sems.at[chunk])
        )
        copies[chunk].start()
    for copy in copies:
        copy.wait()


def normalize(y, squares):
    return pl.pallas_call(
        norm_kernel,
        in_specs=[VMEM] * 5,
        out_specs=ANY,
        out_shape=jax.ShapeDtypeStruct((TOK_DEV, FEATURES), BF16),
        scratch_shapes=[
            pltpu.VMEM((TOK_DEV, FEATURES), BF16),
            pltpu.SemaphoreType.DMA((CHUNKS,)),
        ],
        compiler_params=pltpu.CompilerParams(**PARAMS),
        name="normalize",
    )(y, *squares)


def swap(array, axis, distance, only_up=None):
    count = lax.axis_size(axis)
    route = [
        (low, low ^ distance)
        for low in range(count)
        if only_up is None or not low >> only_up & 1
    ]
    return lax.ppermute(array, axis, route)


def per_device(inputs, state_in, state_out, log_decay, level_weight, skip, norm_gain, resets):
    total, pay, starts, log, far, span, x, b, c, weights = block_states(
        resets, inputs, state_in, state_out, log_decay, level_weight
    )
    one = swap(pay, "seq", 1)
    half, span, lead, one_factor, pay = join_cores(total, span, one)
    within = (resets, skip, x, b, c, log, weights, far, starts, one, one_factor)
    got = [swap(pay, "seq", distance) for distance in (2, 6, 4)]
    parts = inner(0, within, None)
    parts = inner(2, within, parts)
    got, parts = lax.optimization_barrier((got, parts))
    shard, span, lead, two_factor, three_factor, pay, mine = join_chips(
        half, span, lead, (got[0], got[2], got[1])
    )
    four = swap(pay, "seq", 8)
    mine, pay = lax.optimization_barrier((mine, pay))
    other = swap(mine, "seq", 1)
    parts = inner(4, within, parts)
    four, parts = lax.optimization_barrier((four, parts))
    shard, span, lead, four_factor, pay = join(3, shard, span, lead, four)
    five = swap(pay, "seq", 16)
    pay, parts = lax.optimization_barrier((pay, parts))
    parts = inner(6, within, parts)
    five, parts = lax.optimization_barrier((five, parts))
    y, flipped, coef = parts
    both, lead, five_factor, pay = join(4, shard, span, lead, five, four)
    six = swap(pay, "seq", 48)
    both, y = lax.optimization_barrier((both, y))
    both_got = swap(both, "seq", 2)
    (y,) = add_levels((2, 3), False, [mine], [other], [two_factor, three_factor], y, flipped, coef)
    both_got, six, y = lax.optimization_barrier((both_got, six, y))
    six_got = swap(six, "seq", 2)
    mine = gather(2, both, [both_got])
    other = swap(mine, "seq", 1)
    (y,) = add_levels((4, 5), False, [mine], [other], [four_factor, five_factor], y, flipped, coef)
    six_got, y = lax.optimization_barrier((six_got, y))
    mine = gather(1, six, [six_got])
    other = swap(mine, "seq", 1)
    y, squares = add_levels((6,), True, [mine], [other], [lead], y, flipped, coef)
    shares = [squares] + [
        lax.ppermute(squares, "head", [(i, i ^ d) for i in range(4)]) for d in (1, 3, 2)
    ]
    return normalize(flip(y, norm_gain.reshape(1, FEATURES)), shares)


def solution(mesh):
    placed = (
        P("seq", "head"),
        P("seq", None),
        P("seq", None),
        P("head", "seq"),
        P(None, "head", "seq"),
        P("head"),
        P("head"),
        P(),
    )
    return jax.shard_map(
        per_device, mesh=mesh, in_specs=placed, out_specs=P("seq", "head"), check_vma=False
    )
```
